256 devices in a mesh: ctx: 32 (over x, z_hi, core), head: 8 (over y, z_lo).
Axes of the slice: x: 4, y: 4, z: 8 (z_hi: 4, z_lo: 2; z = z_hi * 2 + z_lo), core: 2. Of those that a mesh axis runs over, the one named last changes fastest.
Arguments:
- keys: bfloat16 [16384, 4096], P('ctx', 'head'), may hold values from -6 to 6
- values: bfloat16 [16384, 4096], P('ctx', 'head'), may hold values from -6 to 6
- rates: float32 [8, 16384], P('head', 'ctx'), may hold values from 0.05 to 1
- queries: bfloat16 [16384, 4096], P(('ctx', 'head')), may hold values from -6 to 6
- fast_weights: bfloat16 [8, 3, 512, 512], P('head'), may hold values from -4 to 4
- gate: bfloat16 [16384, 4096], P(('ctx', 'head')), may hold values from -6 to 6
- gain: float32 [4096], replicated, may hold values from 0.1 to 1.9
Outputs:
- layer_out: bfloat16 [16384, 4096], P(('ctx', 'head'))
- new_weights: bfloat16 [8, 3, 512, 512], P('head')
The draws below stay inside these ranges and needn't reach their ends.
All inputs are finite; a program needn't handle non-finite values.
Results may differ from the reference program's by a relative error of at most 0.023.
Values may be sent and summed in bfloat16 or wider, within the bound.
A program may use at most 64 MiB of HBM per device.

```python
import math
import jax
import jax.numpy as jnp
from jax import lax

DH = 512
NS_STEPS = 5
HEADS = 8
D = 4096
TOKENS = 16384


def level_of(rng, dims, cuts, smallest, top_value):
    def one(axis_at, blocks):
        steps = jax.random.uniform(jax.random.fold_in(jax.random.fold_in(rng, 6), axis_at), (blocks,), jnp.float32, smallest / len(cuts), top_value / len(cuts))
        return jnp.repeat(jnp.exp(steps), dims[axis_at] // blocks).reshape((-1,) + (1,) * (len(dims) - axis_at - 1))

    level = one(*cuts[0])
    for cut in cuts[1:]:
        level = level * one(*cut)
    return level


def normal_values(stream_key, shape, deviation, limit, shards=(), held_as=jnp.bfloat16):
    values = deviation * jax.random.normal(stream_key, shape, jnp.float32)
    if shards:
        values = values * level_of(stream_key, shape, shards, -0.22, 0.18)
    return jnp.clip(values, -limit, limit).astype(held_as)


def setup_inputs(seed: int = 0) -> dict:
    streams_of = jax.random.split(jax.random.key(seed), 8)
    return {
        "keys": normal_values(streams_of[0], (TOKENS, D), 1.0, 6.0, ((0, 32), (1, 8))),
        "values": normal_values(streams_of[1], (TOKENS, D), 1.0, 6.0, ((0, 32), (1, 8))),
        "rates": jnp.clip(jnp.exp(math.log(1.0) - 2.9957323 * jax.random.uniform(streams_of[2], (HEADS, TOKENS), jnp.float32) ** level_of(streams_of[2], (HEADS, TOKENS), ((0, 8), (1, 32)), -0.2, 0.2)), 0.05, 1.0),
        "queries": normal_values(streams_of[3], (TOKENS, D), 1.0, 6.0, ((0, 256),)),
        "fast_weights": normal_values(streams_of[4], (HEADS, 3, DH, DH), 1.0, 4.0, ((0, 8),)),
        "gate": normal_values(streams_of[5], (TOKENS, D), 1.0, 6.0, ((0, 256),)),
        "gain": jnp.clip(1.0 + 0.18 * jax.random.normal(streams_of[6], (D,), jnp.float32), 0.1, 1.9),
    }


coef_a = 3.4445
coef_b = -4.775
coef_c = 2.0315

def mat(left, right):
    return jnp.dot(left, right, preferred_element_type=jnp.float32)

def orthogonalize(grad):
    total = jnp.sum(grad * grad)
    iterate = (grad / (jnp.sqrt(total) + 1e-07)).astype(jnp.bfloat16)
    for step in range(NS_STEPS):
        gram = mat(iterate, iterate.T).astype(jnp.bfloat16)
        square = mat(gram, gram)
        poly = (coef_b * gram.astype(jnp.float32) + coef_c * square).astype(jnp.bfloat16)
        iterate = (coef_a * iterate.astype(jnp.float32) + mat(poly, iterate)).astype(jnp.bfloat16)
    return iterate

def head_terms(items):
    key_h, value_h, rate_h, query_h, weight_h = items
    scale = DH ** (-0.5)
    g_one = mat(key_h, weight_h[0]) * scale
    g_three = mat(key_h, weight_h[1]) * scale
    sig = jax.nn.sigmoid(g_one)
    hidden = (g_one * sig * g_three).astype(jnp.bfloat16)
    grad_out = (-(rate_h[:, None] * value_h.astype(jnp.float32))).astype(jnp.bfloat16)
    d_two = mat(hidden.T, grad_out) * scale
    d_hidden = mat(grad_out, weight_h[2].T) * scale
    dg_one = (d_hidden * g_three * sig * (1.0 + g_one * (1.0 - sig))).astype(jnp.bfloat16)
    dg_three = (d_hidden * (g_one * sig)).astype(jnp.bfloat16)
    d_one = mat(key_h.T, dg_one) * scale
    d_three = mat(key_h.T, dg_three) * scale
    grads = [d_one, d_three, d_two]
    updated = []
    for index in range(3):
        direction = orthogonalize(grads[index])
        updated.append((weight_h[index].astype(jnp.float32) - 0.4 * jnp.sqrt(jnp.float32(DH)) * direction.astype(jnp.float32)).astype(jnp.bfloat16))
    new_head = jnp.stack(updated)
    r_one = mat(query_h, weight_h[0]) * scale
    r_three = mat(query_h, weight_h[1]) * scale
    hq = (jax.nn.silu(r_one) * r_three).astype(jnp.bfloat16)
    read = (mat(hq, weight_h[2]) * scale).astype(jnp.bfloat16)
    return (read, new_head)

def reference(keys, values, rates, queries, fast_weights, gate, gain):
    tokens = keys.shape[0]
    heads = fast_weights.shape[0]

    def split(array):
        return array.reshape(tokens, heads, DH).transpose(1, 0, 2)
    read, new_weights = lax.map(head_terms, (split(keys), split(values), rates, split(queries), fast_weights))
    read32 = read.transpose(1, 0, 2).astype(jnp.float32)
    mean_sq = lax.optimization_barrier(jnp.mean(read32 * read32, axis=-1, keepdims=True))
    gate32 = gate.astype(jnp.float32).reshape(tokens, heads, DH)
    normed = read32 * lax.rsqrt(mean_sq + 1e-06) * gain.reshape(heads, DH) * jax.nn.silu(gate32)
    return (normed.reshape(tokens, heads * DH).astype(jnp.bfloat16), new_weights)
```

```python
import functools

import jax
import jax.numpy as jnp
from jax import lax
from jax.experimental import pallas as pl
from jax.experimental.pallas import tpu as pltpu
from jax.sharding import PartitionSpec as P

NS_STEPS = 5
DH = 512
HEADS = 8
SCALE = DH ** (-0.5)
COEF_A, COEF_B, COEF_C = 3.4445, -4.775, 2.0315
F32, BF16 = jnp.float32, jnp.bfloat16
NT = (((1,), (1,)), ((), ()))
TN = (((0,), (0,)), ((), ()))
NN = (((1,), (0,)), ((), ()))


def mat(left, right, dims=NN):
    return lax.dot_general(left, right, dims, preferred_element_type=F32)


def memory_kernel(
    keys, values, rates, queries, weights, gate, gain,
    layer_out, new_weights,
    k_v, v_v, w_v, gate_v, q_buf, r_out, r_in, out_v, nw_v,
    loc, c_recv, part, x_recv, z_buf, full, x_it, gram, dg_v,
    in_sem, out_sem, q_ss, q_rs, r_ss, r_rs, c_ss, c_rs, x_ss, x_rs, z_ss, z_rs, a_ss, a_rs, f_ss, f_rs,
):
    ctx, head = lax.axis_index("ctx"), lax.axis_index("head")
    xi, zi, core = ctx // 8, (ctx // 2) % 4, ctx % 2

    def at(x, z, c):
        return (x * 8 + z * 2 + c, head)

    def x_other(d):
        return (xi + d) % 4

    def z_other(d):
        return (zi + d) % 4

    sibling = at(xi, zi, 1 - core)
    heads_other = [(head + d) % HEADS for d in range(1, HEADS)]

    def remote(src, dst, ss, rs, target):
        return pltpu.make_async_remote_copy(
            src_ref=src, dst_ref=dst, send_sem=ss, recv_sem=rs,
            device_id=target, device_id_type=pl.DeviceIdType.MESH,
        )

    barrier = pltpu.get_barrier_semaphore()
    partners = [sibling] + [at(x_other(d), zi, core) for d in (1, 2, 3)]
    partners += [at(xi, z_other(d), core) for d in (1, 2, 3)] + [(ctx, h) for h in heads_other]
    for partner in partners:
        pl.semaphore_signal(barrier, inc=1, device_id=partner, device_id_type=pl.DeviceIdType.MESH)

    loads = [
        pltpu.make_async_copy(keys, k_v, in_sem.at[0]),
        pltpu.make_async_copy(weights.at[0, 0], w_v.at[0], in_sem.at[1]),
        pltpu.make_async_copy(weights.at[0, 1], w_v.at[1], in_sem.at[2]),
        pltpu.make_async_copy(values, v_v, in_sem.at[3]),
        pltpu.make_async_copy(weights.at[0, 2], w_v.at[2], in_sem.at[4]),
        pltpu.make_async_copy(
            queries.at[:, pl.ds(pl.multiple_of(head * DH, DH), DH)], q_buf.at[head], in_sem.at[5]
        ),
        pltpu.make_async_copy(gate, gate_v, in_sem.at[6]),
    ]
    for load in loads:
        load.start()

    loads[0].wait()
    loads[1].wait()
    g_one = mat(k_v[...], w_v[0]) * SCALE
    loads[2].wait()
    g_three = mat(k_v[...], w_v[1]) * SCALE
    sig = jax.nn.sigmoid(g_one)
    hidden = (g_one * sig * g_three).astype(BF16)
    loads[3].wait()
    rate_col = jnp.broadcast_to(rates[...], (128, DH)).T
    rate_wide = jnp.concatenate([rate_col] * 4, axis=1)
    grad_out = (-(rate_wide * v_v[...].astype(F32))).astype(BF16)
    loc[2] = (mat(hidden, grad_out, TN) * SCALE).astype(BF16)

    core_copies, x_copies, z_copies, a_copies, f_copies = {}, {}, {}, {}, {}

    def core_send(m):
        core_copies[m] = remote(
            loc.at[m, pl.ds(pl.multiple_of((1 - core) * 256, 256), 256)], c_recv.at[m],
            c_ss.at[m], c_rs.at[m], sibling,
        )
        core_copies[m].start()

    def x_send(m):
        core_copies[m].wait_recv()
        mine = loc[m, pl.ds(pl.multiple_of(core * 256, 256), 256), :].astype(F32)
        part[m] = (mine + c_recv[m].astype(F32)).astype(BF16).reshape(4, 64, DH)
        x_copies[m] = []
        for d in (1, 3, 2):
            copy = remote(
                part.at[m, x_other(d)], x_recv.at[m, d - 1], x_ss.at[m, d - 1], x_rs.at[m, d - 1],
                at(x_other(d), zi, core),
            )
            copy.start()
            x_copies[m].append(copy)

    def z_send(m):
        for copy in x_copies[m]:
            copy.wait_recv()
        total = part[m, xi].astype(F32)
        for d in range(3):
            total = total + x_recv[m, d].astype(F32)
        z_buf[m, zi] = total.astype(BF16)
        z_copies[m] = []
        for d in (1, 3, 2):
            copy = remote(
                z_buf.at[m, zi], z_buf.at[m, zi], z_ss.at[m, d - 1], z_rs.at[m, d - 1],
                at(xi, z_other(d), core),
            )
            copy.start()
            z_copies[m].append(copy)

    def forward(m, which, chunk):
        copy = remote(
            full.at[m, core, chunk], full.at[m, core, chunk], f_ss.at[m, which], f_rs.at[m, which], sibling
        )
        copy.start()
        f_copies[m].append(copy)

    def a_send(m):
        for copy in z_copies[m]:
            copy.wait_recv()
        total = z_buf[m, 0].astype(F32)
        for z in range(1, 4):
            total = total + z_buf[m, z].astype(F32)
        full[m, core, xi] = total.astype(BF16)
        a_copies[m] = []
        for d in (1, 3, 2):
            copy = remote(
                full.at[m, core, xi], full.at[m, core, xi], a_ss.at[m, d - 1], a_rs.at[m, d - 1],
                at(x_other(d), zi, core),
            )
            copy.start()
            a_copies[m].append(copy)
        f_copies[m] = []
        forward(m, 0, xi)

    def f_send(m):
        for i, d in enumerate((1, 3, 2)):
            a_copies[m][i].wait_recv()
            forward(m, d, (xi + 4 - d) % 4)

    def gather_end(m):
        for copy in f_copies[m]:
            copy.wait_recv()

    pl.semaphore_wait(barrier, len(partners))
    core_send(2)

    q_copies = []
    for d, h in enumerate(heads_other):
        copy = remote(
            queries.at[:, pl.ds(pl.multiple_of(h * DH, DH), DH)], q_buf.at[head], q_ss.at[d], q_rs.at[d], (ctx, h)
        )
        copy.start()
        q_copies.append(copy)

    loads[4].wait()
    d_hidden = mat(grad_out, w_v[2], NT) * SCALE
    dg_v[0] = (d_hidden * g_three * sig * (1.0 + g_one * (1.0 - sig))).astype(BF16)
    dg_v[1] = (d_hidden * (g_one * sig)).astype(BF16)
    x_send(2)
    loc[0] = (mat(k_v[...], dg_v[0], TN) * SCALE).astype(BF16)
    core_send(0)
    loc[1] = (mat(k_v[...], dg_v[1], TN) * SCALE).astype(BF16)
    core_send(1)
    x_send(0)
    x_send(1)
    z_send(2)

    loads[5].wait()
    for copy in q_copies:
        copy.wait_recv()
    q_rows = q_buf[...].reshape(HEADS * 64, DH)
    r_one = mat(q_rows, w_v[0]) * SCALE
    r_three = mat(q_rows, w_v[1]) * SCALE
    hq = (r_one * jax.nn.sigmoid(r_one) * r_three).astype(BF16)
    r_out[...] = (mat(hq, w_v[2]) * SCALE).astype(BF16).reshape(HEADS, 64, DH)
    z_send(0)
    z_send(1)
    r_copies = []
    for d, h in enumerate(heads_other):
        copy = remote(r_out.at[h], r_in.at[head], r_ss.at[d], r_rs.at[d], (ctx, h))
        copy.start()
        r_copies.append(copy)
    r_in[head] = r_out[head]

    a_send(2)
    a_send(0)
    a_send(1)

    loads[6].wait()
    for copy in r_copies:
        copy.wait_recv()
    for h in range(HEADS):
        cols = slice(h * DH, (h + 1) * DH)
        read = r_in[h].astype(F32)
        mean_sq = jnp.mean(read * read, axis=-1, keepdims=True)
        gated = gate_v[:, cols].astype(F32)
        out_v[:, cols] = (
            read * lax.rsqrt(mean_sq + 1e-06) * gain[:, cols] * (gated * jax.nn.sigmoid(gated))
        ).astype(BF16)
    stores = [pltpu.make_async_copy(out_v, layer_out, out_sem.at[3])]
    stores[0].start()

    def orthogonalise(m):
        grad = full[m].reshape(DH, DH).astype(F32)
        norm = jnp.sqrt(jnp.sum(grad * grad)) + 1e-07
        x_it[m] = (grad / norm).astype(BF16)

        def step(_, carry):
            gram[m] = mat(x_it[m], x_it[m], NT).astype(BF16)
            square = mat(gram[m], gram[m])
            poly = (COEF_B * gram[m].astype(F32) + COEF_C * square).astype(BF16)
            x_it[m] = (COEF_A * x_it[m].astype(F32) + mat(poly, x_it[m])).astype(BF16)
            return carry

        lax.fori_loop(0, NS_STEPS, step, 0)
        step_size = 0.4 * DH ** 0.5
        nw_v[m] = (w_v[m].astype(F32) - step_size * x_it[m].astype(F32)).astype(BF16)
        store = pltpu.make_async_copy(nw_v.at[m], new_weights.at[0, m], out_sem.at[m])
        store.start()
        stores.append(store)

    f_send(2)
    gather_end(2)
    orthogonalise(2)
    f_send(0)
    gather_end(0)
    orthogonalise(0)
    f_send(1)
    gather_end(1)
    orthogonalise(1)

    for group in (x_copies, z_copies, a_copies, f_copies):
        for m in range(3):
            for copy in group[m]:
                copy.wait_send()
    for m in range(3):
        core_copies[m].wait_send()
    for copy in q_copies + r_copies:
        copy.wait_send()
    for store in stores:
        store.wait()


def local(keys, values, rates, queries, fast_weights, gate, gain):
    anywhere = pl.BlockSpec(memory_space=pl.ANY)
    vmem = pl.BlockSpec(memory_space=pltpu.VMEM)
    dma = pltpu.SemaphoreType.DMA
    return pl.pallas_call(
        memory_kernel,
        name="memory_layer",
        out_shape=(
            jax.ShapeDtypeStruct((64, HEADS * DH), BF16),
            jax.ShapeDtypeStruct((1, 3, DH, DH), BF16),
        ),
        in_specs=[anywhere, anywhere, vmem, anywhere, anywhere, anywhere, vmem],
        out_specs=(anywhere, anywhere),
        scratch_shapes=[
            pltpu.VMEM((512, DH), BF16),
            pltpu.VMEM((512, DH), BF16),
            pltpu.VMEM((3, DH, DH), BF16),
            pltpu.VMEM((64, HEADS * DH), BF16),
            pltpu.VMEM((HEADS, 64, DH), BF16),
            pltpu.VMEM((HEADS, 64, DH), BF16),
            pltpu.VMEM((HEADS, 64, DH), BF16),
            pltpu.VMEM((64, HEADS * DH), BF16),
            pltpu.VMEM((3, DH, DH), BF16),
            pltpu.VMEM((3, DH, DH), BF16),
            pltpu.VMEM((3, 256, DH), BF16),
            pltpu.VMEM((3, 4, 64, DH), BF16),
            pltpu.VMEM((3, 3, 64, DH), BF16),
            pltpu.VMEM((3, 4, 64, DH), BF16),
            pltpu.VMEM((3, 2, 4, 64, DH), BF16),
            pltpu.VMEM((3, DH, DH), BF16),
            pltpu.VMEM((3, DH, DH), BF16),
            pltpu.VMEM((2, DH, DH), BF16),
            dma((7,)), dma((4,)),
            dma((7,)), dma((7,)), dma((7,)), dma((7,)),
            dma((3,)), dma((3,)),
            dma((3, 3)), dma((3, 3)), dma((3, 3)), dma((3, 3)), dma((3, 3)), dma((3, 3)),
            dma((3, 4)), dma((3, 4)),
        ],
        compiler_params=pltpu.CompilerParams(
            collective_id=0, has_side_effects=True, vmem_limit_bytes=48 * 2**20
        ),
    )(keys, values, rates, queries, fast_weights, gate, gain.reshape(1, HEADS * DH))


def solution(mesh):
    in_specs = (
        P("ctx", "head"),
        P("ctx", "head"),
        P("head", "ctx"),
        P(("ctx", "head"), None),
        P("head", None, None, None),
        P(("ctx", "head"), None),
        P(),
    )
    out_specs = (P(("ctx", "head"), None), P("head", None, None, None))
    return jax.shard_map(local, mesh=mesh, in_specs=in_specs, out_specs=out_specs, check_vma=False)
```

```python
import functools

import jax
import jax.numpy as jnp
from jax import lax
from jax.experimental import pallas as pl
from jax.experimental.pallas import tpu as pltpu
from jax.sharding import PartitionSpec as P

NS_STEPS = 5
DH = 512
HEADS = 8
SCALE = DH ** (-0.5)
COEF_A, COEF_B, COEF_C = 3.4445, -4.775, 2.0315
F32, BF16 = jnp.float32, jnp.bfloat16
NT = (((1,), (1,)), ((), ()))
TN = (((0,), (0,)), ((), ()))
NN = (((1,), (0,)), ((), ()))


def mat(left, right, dims=NN):
    return lax.dot_general(left, right, dims, preferred_element_type=F32)


SCHEDULE = (
    ("grad_two", 0), ("greet", 0), ("core_send", 2), ("query_send", 0), ("grad_hidden", 0), ("x_send", 2),
    ("grad_one_three", 0), ("core_send", 0), ("grad_one_three", 1), ("core_send", 1), ("x_send", 0), ("x_send", 1),
    ("z_send", 2), ("z_send", 0), ("z_send", 1), ("readout", 0), ("y_send", 0), ("a_send", 2), ("y_send", 1),
    ("a_send", 0), ("a_send", 1), ("read_send", 0), ("f_send", 2), ("normalise", 2), ("orthogonal", 2),
    ("orthogonal", 2), ("orthogonal", 2), ("f_send", 0), ("orthogonal", 2), ("orthogonal", 2), ("orthogonal", 2),
    ("orthogonal", 2), ("orthogonal", 2), ("orthogonal", 2), ("orthogonal", 2), ("orthogonal", 2), ("orthogonal", 2),
    ("f_send", 1), ("orthogonal", 2), ("orthogonal", 2), ("orthogonal", 2), ("update", 2), ("normalise", 0),
    ("normalise", 1), ("orthogonal", 0), ("orthogonal", 1), ("orthogonal", 0), ("orthogonal", 1), ("orthogonal", 0),
    ("orthogonal", 1), ("orthogonal", 0), ("orthogonal", 1), ("orthogonal", 0), ("orthogonal", 1), ("orthogonal", 0),
    ("orthogonal", 1), ("finish_read", 0), ("orthogonal", 0), ("orthogonal", 1), ("orthogonal", 0), ("orthogonal", 1),
    ("orthogonal", 0), ("orthogonal", 1), ("orthogonal", 0), ("orthogonal", 1), ("orthogonal", 0), ("orthogonal", 1),
    ("orthogonal", 0), ("orthogonal", 1), ("orthogonal", 0), ("orthogonal", 1), ("orthogonal", 0), ("orthogonal", 1),
    ("orthogonal", 0), ("orthogonal", 1), ("update", 0), ("update", 1),
)
Z_SCATTER = (0, 1)
HALVES = (slice(0, 256), slice(256, 512))


def orthogonal_step(m, phase, x_it, gram, poly):
    low, high = HALVES
    if phase == 0:
        gram[m, :, low] = mat(x_it[m], x_it[m, low, :], NT).astype(BF16)
        gram[m, high, high] = mat(x_it[m, high], x_it[m, high, :], NT).astype(BF16)
        gram[m, low, high] = gram[m, high, low].T
    elif phase == 1:
        poly[m, :, low] = (
            COEF_B * gram[m, :, low].astype(F32) + COEF_C * mat(gram[m], gram[m, :, low])
        ).astype(BF16)
        poly[m, high, high] = (
            COEF_B * gram[m, high, high].astype(F32) + COEF_C * mat(gram[m, high], gram[m, :, high])
        ).astype(BF16)
        poly[m, low, high] = poly[m, high, low].T
    else:
        for cols in HALVES:
            x_it[m, :, cols] = (
                COEF_A * x_it[m, :, cols].astype(F32) + mat(poly[m], x_it[m, :, cols])
            ).astype(BF16)


def memory_kernel(
    schedule, z_scatter, keys, values, rates, queries, weights, gate, gain,
    layer_out, new_weights,
    k_v, v_v, w_v, rate_v, gate_v, gain_v, q_buf, r_out, r_in,
    loc, c_recv, part, x_recv, z_buf, z_part, z_recv, full, x_it, gram, poly, dg_v,
    in_sem, q_ss, q_rs, r_ss, r_rs, c_ss, c_rs, x_ss, x_rs, z_ss, z_rs, y_ss, y_rs, a_ss, a_rs, f_ss, f_rs,
):
    ctx, head = lax.axis_index("ctx"), lax.axis_index("head")
    xi, zi, core = ctx // 8, (ctx // 2) % 4, ctx % 2

    def at(x, z, c):
        return (x * 8 + z * 2 + c, head)

    def x_other(d):
        return (xi + d) % 4

    def z_other(d):
        return (zi + d) % 4

    sibling = at(xi, zi, 1 - core)
    heads_other = [(head + d) % HEADS for d in range(1, HEADS)]

    def remote(src, dst, ss, rs, target):
        return pltpu.make_async_remote_copy(
            src_ref=src, dst_ref=dst, send_sem=ss, recv_sem=rs,
            device_id=target, device_id_type=pl.DeviceIdType.MESH,
        )

    barrier = pltpu.get_barrier_semaphore()
    partners = [sibling] + [at(x_other(d), zi, core) for d in (1, 2, 3)]
    partners += [at(xi, z_other(d), core) for d in (1, 2, 3)] + [(ctx, h) for h in heads_other]
    for partner in partners:
        pl.semaphore_signal(barrier, inc=1, device_id=partner, device_id_type=pl.DeviceIdType.MESH)

    loads = [
        pltpu.make_async_copy(keys, k_v, in_sem.at[0]),
        pltpu.make_async_copy(weights.at[0, 0], w_v.at[0], in_sem.at[1]),
        pltpu.make_async_copy(weights.at[0, 1], w_v.at[1], in_sem.at[2]),
        pltpu.make_async_copy(values, v_v, in_sem.at[3]),
        pltpu.make_async_copy(weights.at[0, 2], w_v.at[2], in_sem.at[4]),
        pltpu.make_async_copy(
            queries.at[:, pl.ds(pl.multiple_of(head * DH, DH), DH)], q_buf.at[head], in_sem.at[5]
        ),
        pltpu.make_async_copy(gate, gate_v, in_sem.at[6]),
        pltpu.make_async_copy(rates, rate_v, in_sem.at[7]),
        pltpu.make_async_copy(gain, gain_v, in_sem.at[8]),
    ]
    for load in loads:
        load.start()

    live, copies = {}, {}

    def greet(_):
        pl.semaphore_wait(barrier, len(partners))

    def grad_two(_):
        loads[0].wait()
        loads[1].wait()
        g_one = mat(k_v[...], w_v[0]) * SCALE
        loads[2].wait()
        g_three = mat(k_v[...], w_v[1]) * SCALE
        sig = jax.nn.sigmoid(g_one)
        hidden = (g_one * sig * g_three).astype(BF16)
        loads[3].wait()
        loads[7].wait()
        rate_col = jnp.broadcast_to(rate_v[...], (128, DH)).T
        rate_wide = jnp.concatenate([rate_col] * 4, axis=1)
        grad_out = (-(rate_wide * v_v[...].astype(F32))).astype(BF16)
        loc[2] = (mat(hidden, grad_out, TN) * SCALE).astype(BF16)
        live.update(g_one=g_one, g_three=g_three, sig=sig, grad_out=grad_out)

    def grad_hidden(_):
        loads[4].wait()
        g_one, sig = live["g_one"], live["sig"]
        d_hidden = mat(live["grad_out"], w_v[2], NT) * SCALE
        dg_v[0] = (d_hidden * live["g_three"] * sig * (1.0 + g_one * (1.0 - sig))).astype(BF16)
        dg_v[1] = (d_hidden * (g_one * sig)).astype(BF16)

    def grad_one_three(m):
        loc[m] = (mat(k_v[...], dg_v[m], TN) * SCALE).astype(BF16)

    def start(key, copy):
        copy.start()
        copies.setdefault(key, []).append(copy)

    def arrived(key):
        for copy in copies[key]:
            copy.wait_recv()

    def core_send(m):
        start(("c", m), remote(
            loc.at[m, pl.ds(pl.multiple_of((1 - core) * 256, 256), 256)], c_recv.at[m],
            c_ss.at[m], c_rs.at[m], sibling,
        ))

    def x_send(m):
        arrived(("c", m))
        mine = loc[m, pl.ds(pl.multiple_of(core * 256, 256), 256), :].astype(F32)
        part[m] = (mine + c_recv[m].astype(F32)).astype(BF16).reshape(4, 64, DH)
        for d in (1, 3, 2):
            start(("x", m), remote(
                part.at[m, x_other(d)], x_recv.at[m, d - 1], x_ss.at[m, d - 1], x_rs.at[m, d - 1],
                at(x_other(d), zi, core),
            ))

    def z_send(m):
        arrived(("x", m))
        total = part[m, xi].astype(F32)
        for d in range(3):
            total = total + x_recv[m, d].astype(F32)
        if m in z_scatter:
            z_part[m] = total.astype(BF16).reshape(4, 16, DH)
        else:
            z_buf[m, zi] = total.astype(BF16).reshape(4, 16, DH)
        for d in (1, 3, 2):
            if m in z_scatter:
                source, target = z_part.at[m, z_other(d)], z_recv.at[m, d - 1]
            else:
                source, target = z_buf.at[m, zi], z_buf.at[m, zi]
            start(("z", m), remote(source, target, z_ss.at[m, d - 1], z_rs.at[m, d - 1], at(xi, z_other(d), core)))

    def y_send(m):
        arrived(("z", m))
        total = z_part[m, zi].astype(F32)
        for d in range(3):
            total = total + z_recv[m, d].astype(F32)
        full[m, core, xi, zi] = total.astype(BF16)
        block = full.at[m, core, xi, zi]
        for d in (1, 3, 2):
            start(("y", m), remote(block, block, y_ss.at[m, d - 1], y_rs.at[m, d - 1], at(xi, z_other(d), core)))

    def a_send(m):
        if m in z_scatter:
            arrived(("y", m))
        else:
            arrived(("z", m))
            total = z_buf[m, 0].astype(F32)
            for z in range(1, 4):
                total = total + z_buf[m, z].astype(F32)
            full[m, core, xi] = total.astype(BF16)
        block = full.at[m, core, xi]
        for d in (1, 3, 2):
            start(("a", m), remote(block, block, a_ss.at[m, d - 1], a_rs.at[m, d - 1], at(x_other(d), zi, core)))
        start(("f", m), remote(block, block, f_ss.at[m, 0], f_rs.at[m, 0], sibling))

    def f_send(m):
        for i, d in enumerate((1, 3, 2)):
            copies["a", m][i].wait_recv()
            block = full.at[m, core, (xi + 4 - d) % 4]
            start(("f", m), remote(block, block, f_ss.at[m, d], f_rs.at[m, d], sibling))

    def normalise(m):
        arrived(("f", m))
        grad = full[m].reshape(DH, DH).astype(F32)
        norm = jnp.sqrt(jnp.sum(grad * grad)) + 1e-07
        x_it[m] = (grad / norm).astype(BF16)

    def update(m):
        step_size = 0.4 * DH ** 0.5
        new_weights[0, m] = (w_v[m].astype(F32) - step_size * x_it[m].astype(F32)).astype(BF16)

    def query_send(_):
        for d, h in enumerate(heads_other):
            start("q", remote(
                queries.at[:, pl.ds(pl.multiple_of(h * DH, DH), DH)], q_buf.at[head], q_ss.at[d], q_rs.at[d], (ctx, h)
            ))

    def readout(_):
        loads[5].wait()
        arrived("q")
        q_rows = q_buf[...].reshape(HEADS * 64, DH)
        r_one = mat(q_rows, w_v[0]) * SCALE
        r_three = mat(q_rows, w_v[1]) * SCALE
        hq = (r_one * jax.nn.sigmoid(r_one) * r_three).astype(BF16)
        r_out[...] = (mat(hq, w_v[2]) * SCALE).astype(BF16).reshape(HEADS, 64, DH)

    def read_send(_):
        for d, h in enumerate(heads_other):
            start("r", remote(r_out.at[h], r_in.at[head], r_ss.at[d], r_rs.at[d], (ctx, h)))
        r_in[head] = r_out[head]

    def finish_read(_):
        loads[6].wait()
        loads[8].wait()
        arrived("r")
        for h in range(HEADS):
            cols = slice(h * DH, (h + 1) * DH)
            read = r_in[h].astype(F32)
            mean_sq = jnp.mean(read * read, axis=-1, keepdims=True)
            gated = gate_v[:, cols].astype(F32)
            layer_out[:, cols] = (
                read * lax.rsqrt(mean_sq + 1e-06) * gain_v[:, cols] * (gated * jax.nn.sigmoid(gated))
            ).astype(BF16)

    work = {
        "greet": greet, "grad_two": grad_two, "grad_hidden": grad_hidden, "grad_one_three": grad_one_three, "core_send": core_send, "x_send": x_send, "z_send": z_send,
        "y_send": y_send, "a_send": a_send, "f_send": f_send, "normalise": normalise, "update": update, "query_send": query_send, "readout": readout,
        "read_send": read_send, "finish_read": finish_read,
    }
    steps = {0: 0, 1: 0, 2: 0}
    for name, m in schedule:
        if name == "orthogonal":
            orthogonal_step(m, steps[m] % 3, x_it, gram, poly)
            steps[m] += 1
        else:
            work[name](m)

    for group in copies.values():
        for copy in group:
            copy.wait_send()


def local(keys, values, rates, queries, fast_weights, gate, gain):
    hbm = pl.BlockSpec(memory_space=pltpu.HBM)
    vmem = pl.BlockSpec(memory_space=pltpu.VMEM)
    dma = pltpu.SemaphoreType.DMA
    return pl.pallas_call(
        functools.partial(memory_kernel, SCHEDULE, Z_SCATTER),
        name="memory_layer",
        out_shape=(
            jax.ShapeDtypeStruct((64, HEADS * DH), BF16),
            jax.ShapeDtypeStruct((1, 3, DH, DH), BF16),
        ),
        in_specs=[hbm] * 7,
        out_specs=(vmem, vmem),
        scratch_shapes=[
            pltpu.VMEM((512, DH), BF16),
            pltpu.VMEM((512, DH), BF16),
            pltpu.VMEM((3, DH, DH), BF16),
            pltpu.VMEM((1, 512), F32),
            pltpu.VMEM((64, HEADS * DH), BF16),
            pltpu.VMEM((1, HEADS * DH), F32),
            pltpu.VMEM((HEADS, 64, DH), BF16),
            pltpu.VMEM((HEADS, 64, DH), BF16),
            pltpu.VMEM((HEADS, 64, DH), BF16),
            pltpu.VMEM((3, DH, DH), BF16),
            pltpu.VMEM((3, 256, DH), BF16),
            pltpu.VMEM((3, 4, 64, DH), BF16),
            pltpu.VMEM((3, 3, 64, DH), BF16),
            pltpu.VMEM((3, 4, 4, 16, DH), BF16),
            pltpu.VMEM((3, 4, 16, DH), BF16),
            pltpu.VMEM((3, 3, 16, DH), BF16),
            pltpu.VMEM((3, 2, 4, 4, 16, DH), BF16),
            pltpu.VMEM((3, DH, DH), BF16),
            pltpu.VMEM((3, DH, DH), BF16),
            pltpu.VMEM((3, DH, DH), BF16),
            pltpu.VMEM((2, DH, DH), BF16),
            dma((9,)),
            dma((7,)), dma((7,)), dma((7,)), dma((7,)),
            dma((3,)), dma((3,)),
            dma((3, 3)), dma((3, 3)), dma((3, 3)), dma((3, 3)), dma((3, 3)), dma((3, 3)), dma((3, 3)), dma((3, 3)),
            dma((3, 4)), dma((3, 4)),
        ],
        compiler_params=pltpu.CompilerParams(
            collective_id=0, has_side_effects=True, vmem_limit_bytes=48 * 2**20
        ),
    )(keys, values, rates, queries, fast_weights, gate, gain.reshape(1, HEADS * DH))


def solution(mesh):
    in_specs = (
        P("ctx", "head"),
        P("ctx", "head"),
        P("head", "ctx"),
        P(("ctx", "head"), None),
        P("head", None, None, None),
        P(("ctx", "head"), None),
        P(),
    )
    out_specs = (P(("ctx", "head"), None), P("head", None, None, None))
    return jax.shard_map(local, mesh=mesh, in_specs=in_specs, out_specs=out_specs, check_vma=False)
```

```python
import functools

import jax
import jax.numpy as jnp
from jax import lax
from jax.experimental import pallas as pl
from jax.experimental.pallas import tpu as pltpu
from jax.sharding import PartitionSpec as P

NS_STEPS = 5
DH = 512
HEADS = 8
SCALE = DH ** (-0.5)
COEF_A, COEF_B, COEF_C = 3.4445, -4.775, 2.0315
STEP_SIZE = 0.4 * DH ** 0.5
F32, BF16 = jnp.float32, jnp.bfloat16
NT = (((1,), (1,)), ((), ()))
TN = (((0,), (0,)), ((), ()))
NN = (((1,), (0,)), ((), ()))


def mat(left, right, dims=NN):
    return lax.dot_general(left, right, dims, preferred_element_type=F32)


SCHEDULE = (
    ("grad_two", 0), ("greet", 0), ("core_send", 2), ("query_send", 0), ("grad_hidden", 0), ("x_send", 2),
    ("grad_one_three", 0), ("core_send", 0), ("grad_one_three", 1), ("core_send", 1), ("x_send", 0), ("x_send", 1),
    ("z_send", 2), ("z_send", 0), ("z_send", 1), ("readout", 0), ("y_send", 2), ("y_send", 0), ("y_send", 1),
    ("read_send", 0), ("a_send", 2), ("a_send", 0), ("a_send", 1), ("forward_two", 2), ("normalise", 0),
    ("orthogonal", 0), ("orthogonal", 0), ("orthogonal", 0), ("orthogonal", 0), ("orthogonal", 0), ("orthogonal", 0),
    ("orthogonal", 0), ("orthogonal", 0), ("orthogonal", 0), ("orthogonal", 0), ("orthogonal", 0), ("orthogonal", 0),
    ("orthogonal", 0), ("orthogonal", 0), ("orthogonal", 0), ("update", 0), ("read_wait", 0), ("finish_read", 0),
    ("finish_read", 1), ("finish_read", 2), ("finish_read", 3), ("finish_read", 4), ("finish_read", 5),
    ("finish_read", 6), ("finish_read", 7), ("forward_other", 0), ("normalise", 1), ("orthogonal", 1),
    ("orthogonal", 1), ("orthogonal", 1), ("orthogonal", 1), ("orthogonal", 1), ("orthogonal", 1), ("orthogonal", 1),
    ("orthogonal", 1), ("orthogonal", 1), ("orthogonal", 1), ("orthogonal", 1), ("orthogonal", 1), ("orthogonal", 1),
    ("orthogonal", 1), ("update_own", 0), ("update_own", 1),
)
HALVES = (slice(0, 256), slice(256, 512))


def orthogonal_step(m, phase, x_it, gram, poly):
    low, high = HALVES
    if phase == 0:
        gram[m, :, low] = mat(x_it[m], x_it[m, low, :], NT).astype(BF16)
        gram[m, high, high] = mat(x_it[m, high], x_it[m, high, :], NT).astype(BF16)
        gram[m, low, high] = gram[m, high, low].T
    elif phase == 1:
        poly[m, :, low] = (
            COEF_B * gram[m, :, low].astype(F32) + COEF_C * mat(gram[m], gram[m, :, low])
        ).astype(BF16)
        poly[m, high, high] = (
            COEF_B * gram[m, high, high].astype(F32) + COEF_C * mat(gram[m, high], gram[m, :, high])
        ).astype(BF16)
        poly[m, low, high] = poly[m, high, low].T
    else:
        for cols in HALVES:
            x_it[m, :, cols] = (
                COEF_A * x_it[m, :, cols].astype(F32) + mat(poly[m], x_it[m, :, cols])
            ).astype(BF16)


def memory_kernel(
    schedule, keys, values, rates, queries, weights, gate, gain,
    layer_out, new_weights,
    k_v, v_v, w_v, rate_v, gate_v, gain_v, q_buf, r_out, r_in, layer_v, new_v,
    loc, c_recv, part, x_recv, z_part, z_recv, full, x_it, gram, poly, dg_v,
    in_sem, q_ss, q_rs, r_ss, r_rs, c_ss, c_rs, x_ss, x_rs, z_ss, z_rs, y_ss, y_rs, a_ss, a_rs, f_ss, f_rs, e_ss, e_rs, out_sem,
):
    ctx, head = lax.axis_index("ctx"), lax.axis_index("head")
    xi, zi, core = ctx // 8, (ctx // 2) % 4, ctx % 2

    def at(x, z, c):
        return (x * 8 + z * 2 + c, head)

    def x_other(d):
        return (xi + d) % 4

    def z_other(d):
        return (zi + d) % 4

    sibling = at(xi, zi, 1 - core)
    heads_other = [(head + d) % HEADS for d in range(1, HEADS)]

    def remote(src, dst, ss, rs, target):
        return pltpu.make_async_remote_copy(
            src_ref=src, dst_ref=dst, send_sem=ss, recv_sem=rs,
            device_id=target, device_id_type=pl.DeviceIdType.MESH,
        )

    barrier = pltpu.get_barrier_semaphore()
    partners = [sibling] + [at(x_other(d), zi, core) for d in (1, 2, 3)]
    partners += [at(xi, z_other(d), core) for d in (1, 2, 3)] + [(ctx, h) for h in heads_other]
    for partner in partners:
        pl.semaphore_signal(barrier, inc=1, device_id=partner, device_id_type=pl.DeviceIdType.MESH)

    loads = [
        pltpu.make_async_copy(keys, k_v, in_sem.at[0]),
        pltpu.make_async_copy(weights.at[0, 0], w_v.at[0], in_sem.at[1]),
        pltpu.make_async_copy(weights.at[0, 1], w_v.at[1], in_sem.at[2]),
        pltpu.make_async_copy(values, v_v, in_sem.at[3]),
        pltpu.make_async_copy(weights.at[0, 2], w_v.at[2], in_sem.at[4]),
        pltpu.make_async_copy(
            queries.at[:, pl.ds(pl.multiple_of(head * DH, DH), DH)], q_buf.at[head], in_sem.at[5]
        ),
        pltpu.make_async_copy(gate, gate_v, in_sem.at[6]),
        pltpu.make_async_copy(rates, rate_v, in_sem.at[7]),
        pltpu.make_async_copy(gain, gain_v, in_sem.at[8]),
    ]
    for load in loads:
        load.start()

    live, copies, stores = {}, {}, []

    def greet(_):
        pl.semaphore_wait(barrier, len(partners))

    def grad_two(_):
        loads[0].wait()
        loads[1].wait()
        g_one = mat(k_v[...], w_v[0]) * SCALE
        loads[2].wait()
        g_three = mat(k_v[...], w_v[1]) * SCALE
        sig = jax.nn.sigmoid(g_one)
        hidden = (g_one * sig * g_three).astype(BF16)
        loads[3].wait()
        loads[7].wait()
        rate_col = jnp.broadcast_to(rate_v[...], (128, DH)).T
        rate_wide = jnp.concatenate([rate_col] * 4, axis=1)
        grad_out = (-(rate_wide * v_v[...].astype(F32))).astype(BF16)
        loc[2] = (mat(hidden, grad_out, TN) * SCALE).astype(BF16)
        live.update(g_one=g_one, g_three=g_three, sig=sig, grad_out=grad_out)

    def grad_hidden(_):
        loads[4].wait()
        g_one, sig = live["g_one"], live["sig"]
        d_hidden = mat(live["grad_out"], w_v[2], NT) * SCALE
        dg_v[0] = (d_hidden * live["g_three"] * sig * (1.0 + g_one * (1.0 - sig))).astype(BF16)
        dg_v[1] = (d_hidden * (g_one * sig)).astype(BF16)

    def grad_one_three(m):
        loc[m] = (mat(k_v[...], dg_v[m], TN) * SCALE).astype(BF16)

    def start(key, copy):
        copy.start()
        copies.setdefault(key, []).append(copy)

    def store(source, target, i):
        copy = pltpu.make_async_copy(source, target, out_sem.at[i])
        copy.start()
        stores.append(copy)

    def arrived(key):
        for copy in copies[key]:
            copy.wait_recv()

    def core_send(m):
        start(("c", m), remote(
            loc.at[m, pl.ds(pl.multiple_of((1 - core) * 256, 256), 256)], c_recv.at[m],
            c_ss.at[m], c_rs.at[m], sibling,
        ))

    def x_send(m):
        arrived(("c", m))
        mine = loc[m, pl.ds(pl.multiple_of(core * 256, 256), 256), :].astype(F32)
        part[m] = (mine + c_recv[m].astype(F32)).astype(BF16).reshape(4, 64, DH)
        for d in (1, 3, 2):
            start(("x", m), remote(
                part.at[m, x_other(d)], x_recv.at[m, d - 1], x_ss.at[m, d - 1], x_rs.at[m, d - 1],
                at(x_other(d), zi, core),
            ))

    def z_send(m):
        arrived(("x", m))
        total = part[m, xi].astype(F32)
        for d in range(3):
            total = total + x_recv[m, d].astype(F32)
        z_part[m] = total.astype(BF16).reshape(4, 16, DH)
        for d in (1, 3, 2):
            start(("z", m), remote(
                z_part.at[m, z_other(d)], z_recv.at[m, d - 1], z_ss.at[m, d - 1], z_rs.at[m, d - 1],
                at(xi, z_other(d), core),
            ))

    def y_send(m):
        arrived(("z", m))
        total = z_part[m, zi].astype(F32)
        for d in range(3):
            total = total + z_recv[m, d].astype(F32)
        full[m, core, xi, zi] = total.astype(BF16)
        block = full.at[m, core, xi, zi]
        for d in (1, 3, 2):
            start(("y", m), remote(block, block, y_ss.at[m, d - 1], y_rs.at[m, d - 1], at(xi, z_other(d), core)))

    def a_send(m):
        arrived(("y", m))
        block = full.at[m, core, xi]
        for d in (1, 3, 2):
            start(("a", m), remote(block, block, a_ss.at[m, d - 1], a_rs.at[m, d - 1], at(x_other(d), zi, core)))
        if m == 2:
            start(("f", m), remote(block, block, f_ss.at[0], f_rs.at[0], sibling))

    def forward_two(_):
        for i, d in enumerate((1, 3, 2)):
            copies["a", 2][i].wait_recv()
            block = full.at[2, core, (xi + 4 - d) % 4]
            start(("f", 2), remote(block, block, f_ss.at[d], f_rs.at[d], sibling))

    def forward_other(_):
        arrived(("a", 0))
        arrived(("a", 1))
        block = full.at[1 - core, core]
        start("e", remote(block, block, e_ss.at[0], e_rs.at[0], sibling))

    def normalise(slot):
        arrived(("f", 2) if slot == 0 else "e")
        grad = full[2 if slot == 0 else core].reshape(DH, DH).astype(F32)
        norm = jnp.sqrt(jnp.sum(grad * grad)) + 1e-07
        x_it[slot] = (grad / norm).astype(BF16)

    def update(_):
        new_v[2] = (w_v[2].astype(F32) - STEP_SIZE * x_it[0].astype(F32)).astype(BF16)
        store(new_v.at[2], new_weights.at[0, 2], 0)

    def update_own(half):
        cols = HALVES[half]
        last = (COEF_A * x_it[1, :, cols].astype(F32) + mat(poly[1], x_it[1, :, cols])).astype(BF16)
        new_v[core, :, cols] = (w_v[core, :, cols].astype(F32) - STEP_SIZE * last.astype(F32)).astype(BF16)
        block = new_v.at[core, :, cols]
        target = new_weights.at[0, core, :, cols]
        start("e", remote(block, target, e_ss.at[1 + half], e_rs.at[1 + half], sibling))
        store(block, target, 1 + half)

    def query_send(_):
        for d, h in enumerate(heads_other):
            start("q", remote(
                queries.at[:, pl.ds(pl.multiple_of(h * DH, DH), DH)], q_buf.at[head], q_ss.at[d], q_rs.at[d], (ctx, h)
            ))

    def readout(_):
        loads[5].wait()
        arrived("q")
        q_rows = q_buf[...].reshape(HEADS * 64, DH)
        r_one = mat(q_rows, w_v[0]) * SCALE
        r_three = mat(q_rows, w_v[1]) * SCALE
        hq = (r_one * jax.nn.sigmoid(r_one) * r_three).astype(BF16)
        r_out[...] = (mat(hq, w_v[2]) * SCALE).astype(BF16).reshape(HEADS, 64, DH)

    def read_send(_):
        for d, h in enumerate(heads_other):
            start("r", remote(r_out.at[h], r_in.at[head], r_ss.at[d], r_rs.at[d], (ctx, h)))
        r_in[head] = r_out[head]

    def read_wait(_):
        loads[6].wait()
        loads[8].wait()
        arrived("r")

    def finish_read(h):
        cols = slice(h * DH, (h + 1) * DH)
        read = r_in[h].astype(F32)
        mean_sq = jnp.mean(read * read, axis=-1, keepdims=True)
        gated = gate_v[:, cols].astype(F32)
        layer_v[:, cols] = (
            read * lax.rsqrt(mean_sq + 1e-06) * gain_v[:, cols] * (gated * jax.nn.sigmoid(gated))
        ).astype(BF16)
        if h == HEADS - 1:
            store(layer_v, layer_out, 3)

    work = {
        "greet": greet, "grad_two": grad_two, "grad_hidden": grad_hidden, "grad_one_three": grad_one_three, "core_send": core_send, "x_send": x_send, "z_send": z_send,
        "y_send": y_send, "a_send": a_send, "forward_two": forward_two, "forward_other": forward_other, "normalise": normalise, "update": update, "update_own": update_own, "read_wait": read_wait, "query_send": query_send, "readout": readout,
        "read_send": read_send, "finish_read": finish_read,
    }
    steps = [0, 0]
    for name, m in schedule:
        if name == "orthogonal":
            orthogonal_step(m, steps[m] % 3, x_it, gram, poly)
            steps[m] += 1
        else:
            work[name](m)

    for copy in copies["e"][1:]:
        copy.wait_recv()
    for group in copies.values():
        for copy in group:
            copy.wait_send()
    for copy in stores:
        copy.wait()


def local(keys, values, rates, queries, fast_weights, gate, gain):
    hbm = pl.BlockSpec(memory_space=pltpu.HBM)
    dma = pltpu.SemaphoreType.DMA
    return pl.pallas_call(
        functools.partial(memory_kernel, SCHEDULE),
        name="memory_layer",
        out_shape=(
            jax.ShapeDtypeStruct((64, HEADS * DH), BF16),
            jax.ShapeDtypeStruct((1, 3, DH, DH), BF16),
        ),
        in_specs=[hbm] * 7,
        out_specs=(hbm, hbm),
        scratch_shapes=[
            pltpu.VMEM((512, DH), BF16),
            pltpu.VMEM((512, DH), BF16),
            pltpu.VMEM((3, DH, DH), BF16),
            pltpu.VMEM((1, 512), F32),
            pltpu.VMEM((64, HEADS * DH), BF16),
            pltpu.VMEM((1, HEADS * DH), F32),
            pltpu.VMEM((HEADS, 64, DH), BF16),
            pltpu.VMEM((HEADS, 64, DH), BF16),
            pltpu.VMEM((HEADS, 64, DH), BF16),
            pltpu.VMEM((64, HEADS * DH), BF16),
            pltpu.VMEM((3, DH, DH), BF16),
            pltpu.VMEM((3, DH, DH), BF16),
            pltpu.VMEM((3, 256, DH), BF16),
            pltpu.VMEM((3, 4, 64, DH), BF16),
            pltpu.VMEM((3, 3, 64, DH), BF16),
            pltpu.VMEM((3, 4, 16, DH), BF16),
            pltpu.VMEM((3, 3, 16, DH), BF16),
            pltpu.VMEM((3, 2, 4, 4, 16, DH), BF16),
            pltpu.VMEM((2, DH, DH), BF16),
            pltpu.VMEM((2, DH, DH), BF16),
            pltpu.VMEM((2, DH, DH), BF16),
            pltpu.VMEM((2, DH, DH), BF16),
            dma((9,)),
            dma((7,)), dma((7,)), dma((7,)), dma((7,)),
            dma((3,)), dma((3,)),
            dma((3, 3)), dma((3, 3)), dma((3, 3)), dma((3, 3)), dma((3, 3)), dma((3, 3)), dma((3, 3)), dma((3, 3)),
            dma((4,)), dma((4,)), dma((3,)), dma((3,)), dma((4,)),
        ],
        compiler_params=pltpu.CompilerParams(
            collective_id=0, has_side_effects=True, vmem_limit_bytes=60 * 2**20
        ),
    )(keys, values, rates, queries, fast_weights, gate, gain.reshape(1, HEADS * DH))


def solution(mesh):
    in_specs = (
        P("ctx", "head"),
        P("ctx", "head"),
        P("head", "ctx"),
        P(("ctx", "head"), None),
        P("head", None, None, None),
        P(("ctx", "head"), None),
        P(),
    )
    out_specs = (P(("ctx", "head"), None), P("head", None, None, None))
    return jax.shard_map(local, mesh=mesh, in_specs=in_specs, out_specs=out_specs, check_vma=False)
```

```python
import functools

import jax
import jax.numpy as jnp
from jax import lax
from jax.experimental import pallas as pl
from jax.experimental.pallas import tpu as pltpu
from jax.sharding import PartitionSpec as P

NS_STEPS = 5
DH = 512
HEADS = 8
SCALE = DH ** (-0.5)
COEF_A, COEF_B, COEF_C = 3.4445, -4.775, 2.0315
STEP_SIZE = 0.4 * DH ** 0.5
F32, BF16 = jnp.float32, jnp.bfloat16
NT = (((1,), (1,)), ((), ()))
TN = (((0,), (0,)), ((), ()))
NN = (((1,), (0,)), ((), ()))


def mat(left, right, dims=NN):
    return lax.dot_general(left, right, dims, preferred_element_type=F32)


SCHEDULE = (
    ("grad_two", 0), ("greet", 0), ("core_send", 2), ("query_send", 0), ("grad_hidden", 0), ("x_send", 2),
    ("grad_one_three", 0), ("core_send", 0), ("core_send", 1), ("grad_one_three", 1), ("x_send", 0), ("x_send", 1),
    ("z_send", 2), ("z_send", 0), ("z_send", 1), ("readout", 0), ("y_send", 2), ("y_send", 0), ("y_send", 1),
    ("read_send", 0), ("a_send", 2), ("a_send", 0), ("a_send", 1), ("forward_two", 2), ("normalise", 0),
    ("orthogonal", 0), ("orthogonal", 0), ("orthogonal", 0), ("orthogonal", 0), ("orthogonal", 0), ("orthogonal", 0),
    ("orthogonal", 0), ("orthogonal", 0), ("orthogonal", 0), ("orthogonal", 0), ("orthogonal", 0), ("orthogonal", 0),
    ("orthogonal", 0), ("orthogonal", 0), ("orthogonal", 0), ("update", 0), ("read_wait", 0), ("finish_read", 0),
    ("finish_read", 1), ("finish_read", 2), ("finish_read", 3), ("finish_read", 4), ("finish_read", 5),
    ("finish_read", 6), ("finish_read", 7), ("normalise", 1), ("orthogonal", 1), ("orthogonal", 1), ("orthogonal", 1),
    ("orthogonal", 1), ("orthogonal", 1), ("orthogonal", 1), ("orthogonal", 1), ("orthogonal", 1), ("orthogonal", 1),
    ("orthogonal", 1), ("orthogonal", 1), ("orthogonal", 1), ("orthogonal", 1), ("orthogonal", 1), ("update_own", 0),
    ("update_own", 1),
)
HALVES = (slice(0, 256), slice(256, 512))


def orthogonal_step(m, phase, x_it, gram, poly):
    low, high = HALVES
    if phase == 0:
        gram[m, :, low] = mat(x_it[m], x_it[m, low, :], NT).astype(BF16)
        gram[m, high, high] = mat(x_it[m, high], x_it[m, high, :], NT).astype(BF16)
        gram[m, low, high] = gram[m, high, low].T
    elif phase == 1:
        poly[m, :, low] = (
            COEF_B * gram[m, :, low].astype(F32) + COEF_C * mat(gram[m], gram[m, :, low])
        ).astype(BF16)
        poly[m, high, high] = (
            COEF_B * gram[m, high, high].astype(F32) + COEF_C * mat(gram[m, high], gram[m, :, high])
        ).astype(BF16)
        poly[m, low, high] = poly[m, high, low].T
    else:
        for cols in HALVES:
            x_it[m, :, cols] = (
                COEF_A * x_it[m, :, cols].astype(F32) + mat(poly[m], x_it[m, :, cols])
            ).astype(BF16)


def memory_kernel(
    schedule, keys, values, rates, queries, weights, gate, gain,
    layer_out, new_weights,
    k_v, v_v, w_v, rate_v, gate_v, gain_v, q_buf, r_out, r_in,
    loc, c_recv, part, x_recv, z_part, z_recv, full, x_it, gram, poly, dg_v,
    in_sem, q_ss, q_rs, r_ss, r_rs, c_ss, c_rs, x_ss, x_rs, z_ss, z_rs, y_ss, y_rs, a_ss, a_rs, f_ss, f_rs, e_ss, e_rs,
):
    ctx, head = lax.axis_index("ctx"), lax.axis_index("head")
    xi, zi, core = ctx // 8, (ctx // 2) % 4, ctx % 2

    def at(x, z, c):
        return (x * 8 + z * 2 + c, head)

    def x_other(d):
        return (xi + d) % 4

    def z_other(d):
        return (zi + d) % 4

    sibling = at(xi, zi, 1 - core)
    heads_other = [(head + d) % HEADS for d in range(1, HEADS)]

    def remote(src, dst, ss, rs, target):
        return pltpu.make_async_remote_copy(
            src_ref=src, dst_ref=dst, send_sem=ss, recv_sem=rs,
            device_id=target, device_id_type=pl.DeviceIdType.MESH,
        )

    barrier = pltpu.get_barrier_semaphore()
    partners = [sibling] + [at(x_other(d), zi, core) for d in (1, 2, 3)]
    partners += [at(xi, z_other(d), core) for d in (1, 2, 3)] + [(ctx, h) for h in heads_other]
    for partner in partners:
        pl.semaphore_signal(barrier, inc=1, device_id=partner, device_id_type=pl.DeviceIdType.MESH)

    loads = [
        pltpu.make_async_copy(keys, k_v, in_sem.at[0]),
        pltpu.make_async_copy(weights.at[0, 0], w_v.at[0], in_sem.at[1]),
        pltpu.make_async_copy(weights.at[0, 1], w_v.at[1], in_sem.at[2]),
        pltpu.make_async_copy(values, v_v, in_sem.at[3]),
        pltpu.make_async_copy(weights.at[0, 2], w_v.at[2], in_sem.at[4]),
        pltpu.make_async_copy(
            queries.at[:, pl.ds(pl.multiple_of(head * DH, DH), DH)], q_buf.at[head], in_sem.at[5]
        ),
        pltpu.make_async_copy(gate, gate_v, in_sem.at[6]),
        pltpu.make_async_copy(rates, rate_v, in_sem.at[7]),
        pltpu.make_async_copy(gain, gain_v, in_sem.at[8]),
    ]
    for load in loads:
        load.start()

    live, copies = {}, {}

    def greet(_):
        pl.semaphore_wait(barrier, len(partners))

    def grad_two(_):
        loads[0].wait()
        loads[1].wait()
        g_one = mat(k_v[...], w_v[0]) * SCALE
        loads[2].wait()
        g_three = mat(k_v[...], w_v[1]) * SCALE
        sig = jax.nn.sigmoid(g_one)
        hidden = (g_one * sig * g_three).astype(BF16)
        loads[3].wait()
        loads[7].wait()
        rate_col = jnp.broadcast_to(rate_v[...], (128, DH)).T
        rate_wide = jnp.concatenate([rate_col] * 4, axis=1)
        grad_out = (-(rate_wide * v_v[...].astype(F32))).astype(BF16)
        loc[2] = (mat(hidden, grad_out, TN) * SCALE).astype(BF16)
        live.update(g_one=g_one, g_three=g_three, sig=sig, grad_out=grad_out)

    def grad_hidden(_):
        loads[4].wait()
        g_one, sig = live["g_one"], live["sig"]
        d_hidden = mat(live["grad_out"], w_v[2], NT) * SCALE
        dg_v[0] = (d_hidden * live["g_three"] * sig * (1.0 + g_one * (1.0 - sig))).astype(BF16)
        dg_v[1] = (d_hidden * (g_one * sig)).astype(BF16)

    def grad_one_three(mine):
        m = core if mine else 1 - core
        loc[m] = (mat(k_v[...], dg_v[m], TN) * SCALE).astype(BF16)

    def start(key, copy):
        copy.start()
        copies.setdefault(key, []).append(copy)

    def arrived(key):
        for copy in copies[key]:
            copy.wait_recv()

    def rows_of(piece, c):
        if piece == 2:
            return loc.at[2, pl.ds(pl.multiple_of(c * 256, 256), 256)]
        return loc.at[c, pl.ds(piece * 256, 256)]

    def core_send(m):
        start(("c", m), remote(rows_of(m, 1 - core), c_recv.at[m], c_ss.at[m], c_rs.at[m], sibling))

    def block_of(piece, *at_block):
        return full.at[(0, core, *at_block) if piece == 2 else (1, piece, *at_block)]

    def x_send(m):
        arrived(("c", m))
        mine = rows_of(m, core)[...].astype(F32)
        part[m] = (mine + c_recv[m].astype(F32)).astype(BF16).reshape(4, 64, DH)
        for d in (1, 3, 2):
            start(("x", m), remote(
                part.at[m, x_other(d)], x_recv.at[m, d - 1], x_ss.at[m, d - 1], x_rs.at[m, d - 1],
                at(x_other(d), zi, core),
            ))

    def z_send(m):
        arrived(("x", m))
        total = part[m, xi].astype(F32)
        for d in range(3):
            total = total + x_recv[m, d].astype(F32)
        z_part[m] = total.astype(BF16).reshape(4, 16, DH)
        for d in (1, 3, 2):
            start(("z", m), remote(
                z_part.at[m, z_other(d)], z_recv.at[m, d - 1], z_ss.at[m, d - 1], z_rs.at[m, d - 1],
                at(xi, z_other(d), core),
            ))

    def y_send(m):
        arrived(("z", m))
        total = z_part[m, zi].astype(F32)
        for d in range(3):
            total = total + z_recv[m, d].astype(F32)
        block = block_of(m, xi, zi)
        block[...] = total.astype(BF16)
        for d in (1, 3, 2):
            start(("y", m), remote(block, block, y_ss.at[m, d - 1], y_rs.at[m, d - 1], at(xi, z_other(d), core)))

    def a_send(m):
        arrived(("y", m))
        block = block_of(m, xi)
        for d in (1, 3, 2):
            start(("a", m), remote(block, block, a_ss.at[m, d - 1], a_rs.at[m, d - 1], at(x_other(d), zi, core)))
        if m == 2:
            start(("f", m), remote(block, block, f_ss.at[0], f_rs.at[0], sibling))

    def forward_two(_):
        for i, d in enumerate((1, 3, 2)):
            copies["a", 2][i].wait_recv()
            block = block_of(2, (xi + 4 - d) % 4)
            start(("f", 2), remote(block, block, f_ss.at[d], f_rs.at[d], sibling))

    def normalise(slot):
        for key in (("f", 2),) if slot == 0 else (("a", 0), ("a", 1)):
            arrived(key)
        grad = full[slot].reshape(DH, DH).astype(F32)
        norm = jnp.sqrt(jnp.sum(grad * grad)) + 1e-07
        x_it[slot] = (grad / norm).astype(BF16)

    def update(_):
        new_weights[0, 2] = (w_v[2].astype(F32) - STEP_SIZE * x_it[0].astype(F32)).astype(BF16)

    def update_own(half):
        cols = HALVES[half]
        last = (COEF_A * x_it[1, :, cols].astype(F32) + mat(poly[1], x_it[1, :, cols])).astype(BF16)
        new_weights[0, core, :, cols] = (w_v[core, :, cols].astype(F32) - STEP_SIZE * last.astype(F32)).astype(BF16)
        block = new_weights.at[0, core, :, cols]
        start("e", remote(block, block, e_ss.at[half], e_rs.at[half], sibling))

    def query_send(_):
        for d, h in enumerate(heads_other):
            start("q", remote(
                queries.at[:, pl.ds(pl.multiple_of(h * DH, DH), DH)], q_buf.at[head], q_ss.at[d], q_rs.at[d], (ctx, h)
            ))

    def readout(_):
        loads[5].wait()
        arrived("q")
        q_rows = q_buf[...].reshape(HEADS * 64, DH)
        r_one = mat(q_rows, w_v[0]) * SCALE
        r_three = mat(q_rows, w_v[1]) * SCALE
        hq = (r_one * jax.nn.sigmoid(r_one) * r_three).astype(BF16)
        r_out[...] = (mat(hq, w_v[2]) * SCALE).astype(BF16).reshape(HEADS, 64, DH)

    def read_send(_):
        for d, h in enumerate(heads_other):
            start("r", remote(r_out.at[h], r_in.at[head], r_ss.at[d], r_rs.at[d], (ctx, h)))
        r_in[head] = r_out[head]

    def read_wait(_):
        loads[6].wait()
        loads[8].wait()
        arrived("r")

    def finish_read(h):
        cols = slice(h * DH, (h + 1) * DH)
        read = r_in[h].astype(F32)
        mean_sq = jnp.mean(read * read, axis=-1, keepdims=True)
        gated = gate_v[:, cols].astype(F32)
        layer_out[:, cols] = (
            read * lax.rsqrt(mean_sq + 1e-06) * gain_v[:, cols] * (gated * jax.nn.sigmoid(gated))
        ).astype(BF16)

    work = {
        "greet": greet, "grad_two": grad_two, "grad_hidden": grad_hidden, "grad_one_three": grad_one_three, "core_send": core_send, "x_send": x_send, "z_send": z_send,
        "y_send": y_send, "a_send": a_send, "forward_two": forward_two, "normalise": normalise, "update": update, "update_own": update_own, "read_wait": read_wait, "query_send": query_send, "readout": readout,
        "read_send": read_send, "finish_read": finish_read,
    }
    steps = [0, 0]
    for name, m in schedule:
        if name == "orthogonal":
            orthogonal_step(m, steps[m] % 3, x_it, gram, poly)
            steps[m] += 1
        else:
            work[name](m)

    arrived("e")
    for group in copies.values():
        for copy in group:
            copy.wait_send()


def local(keys, values, rates, queries, fast_weights, gate, gain):
    operands = (keys, values, rates, queries, fast_weights, gate, gain.reshape(1, HEADS * DH))
    vmem = pl.BlockSpec(memory_space=pltpu.VMEM)
    hbm = pl.BlockSpec(memory_space=pltpu.HBM)
    dma = pltpu.SemaphoreType.DMA
    return pl.pallas_call(
        functools.partial(memory_kernel, SCHEDULE),
        name="memory_layer",
        out_shape=(
            pltpu.VMEM((64, HEADS * DH), BF16),
            pltpu.VMEM((1, 3, DH, DH), BF16),
        ),
        in_specs=[hbm] * 7,
        out_specs=(vmem, vmem),
        scratch_shapes=[
            pltpu.VMEM((512, DH), BF16),
            pltpu.VMEM((512, DH), BF16),
            pltpu.VMEM((3, DH, DH), BF16),
            pltpu.VMEM((1, 512), F32),
            pltpu.VMEM((64, HEADS * DH), BF16),
            pltpu.VMEM((1, HEADS * DH), F32),
            pltpu.VMEM((HEADS, 64, DH), BF16),
            pltpu.VMEM((HEADS, 64, DH), BF16),
            pltpu.VMEM((HEADS, 64, DH), BF16),
            pltpu.VMEM((3, DH, DH), BF16),
            pltpu.VMEM((3, 256, DH), BF16),
            pltpu.VMEM((3, 4, 64, DH), BF16),
            pltpu.VMEM((3, 3, 64, DH), BF16),
            pltpu.VMEM((3, 4, 16, DH), BF16),
            pltpu.VMEM((3, 3, 16, DH), BF16),
            pltpu.VMEM((2, 2, 4, 4, 16, DH), BF16),
            pltpu.VMEM((2, DH, DH), BF16),
            pltpu.VMEM((2, DH, DH), BF16),
            pltpu.VMEM((2, DH, DH), BF16),
            pltpu.VMEM((2, DH, DH), BF16),
            dma((9,)),
            dma((7,)), dma((7,)), dma((7,)), dma((7,)),
            dma((3,)), dma((3,)),
            dma((3, 3)), dma((3, 3)), dma((3, 3)), dma((3, 3)), dma((3, 3)), dma((3, 3)), dma((3, 3)), dma((3, 3)),
            dma((4,)), dma((4,)), dma((2,)), dma((2,)),
        ],
        compiler_params=pltpu.CompilerParams(
            collective_id=0, has_side_effects=True, vmem_limit_bytes=44 * 2**20
        ),
    )(*(pltpu.with_memory_space_constraint(operand, pltpu.HBM) for operand in operands))


def solution(mesh):
    in_specs = (
        P("ctx", "head"),
        P("ctx", "head"),
        P("head", "ctx"),
        P(("ctx", "head"), None),
        P("head", None, None, None),
        P(("ctx", "head"), None),
        P(),
    )
    out_specs = (P(("ctx", "head"), None), P("head", None, None, None))
    return jax.shard_map(local, mesh=mesh, in_specs=in_specs, out_specs=out_specs, check_vma=False)
```

```python
import functools

import jax
import jax.numpy as jnp
from jax import lax
from jax.experimental import pallas as pl
from jax.experimental.pallas import tpu as pltpu
from jax.sharding import PartitionSpec as P

NS_STEPS = 5
DH = 512
HEADS = 8
SCALE = DH ** (-0.5)
COEF_A, COEF_B, COEF_C = 3.4445, -4.775, 2.0315
STEP_SIZE = 0.4 * DH ** 0.5
F32, BF16 = jnp.float32, jnp.bfloat16
NT = (((1,), (1,)), ((), ()))
TN = (((0,), (0,)), ((), ()))
NN = (((1,), (0,)), ((), ()))


def mat(left, right, dims=NN):
    return lax.dot_general(left, right, dims, preferred_element_type=F32)


SCHEDULE = (
    ("grad_two", 0), ("greet", 0), ("core_send", 2), ("query_send", 0), ("grad_two", 1), ("x_send", 2),
    ("grad_hidden", 0), ("grad_hidden", 1), ("grad_one_three", 0), ("core_send", 0), ("core_send", 1),
    ("grad_one_three", 1), ("x_send", 0), ("x_send", 1), ("z_send", 2), ("z_send", 0), ("z_send", 1), ("readout", 0),
    ("y_send", 2), ("y_send", 0), ("y_send", 1), ("read_send", 0), ("a_send", 2), ("a_send", 0), ("a_send", 1),
    ("forward_two", 2), ("normalise", 0), ("orthogonal", 0), ("orthogonal", 0), ("orthogonal", 0), ("orthogonal", 0),
    ("orthogonal", 0), ("orthogonal", 0), ("orthogonal", 0), ("orthogonal", 0), ("orthogonal", 0), ("orthogonal", 0),
    ("orthogonal", 0), ("orthogonal", 0), ("orthogonal", 0), ("orthogonal", 0), ("orthogonal", 0), ("update", 0),
    ("read_wait", 0), ("finish_read", 0), ("finish_read", 1), ("finish_read", 2), ("finish_read", 3),
    ("finish_read", 4), ("finish_read", 5), ("finish_read", 6), ("finish_read", 7), ("normalise", 1),
    ("orthogonal", 1), ("orthogonal", 1), ("orthogonal", 1), ("orthogonal", 1), ("orthogonal", 1), ("orthogonal", 1),
    ("orthogonal", 1), ("orthogonal", 1), ("orthogonal", 1), ("orthogonal", 1), ("orthogonal", 1), ("orthogonal", 1),
    ("orthogonal", 1), ("orthogonal", 1), ("update_own", 0), ("update_own", 1),
)
HALVES = (slice(0, 256), slice(256, 512))


def orthogonal_step(m, phase, x_it, gram, poly):
    low, high = HALVES
    if phase == 0:
        gram[m, :, low] = mat(x_it[m], x_it[m, low, :], NT).astype(BF16)
        gram[m, high, high] = mat(x_it[m, high], x_it[m, high, :], NT).astype(BF16)
        gram[m, low, high] = gram[m, high, low].T
    elif phase == 1:
        poly[m, :, low] = (
            COEF_B * gram[m, :, low].astype(F32) + COEF_C * mat(gram[m], gram[m, :, low])
        ).astype(BF16)
        poly[m, high, high] = (
            COEF_B * gram[m, high, high].astype(F32) + COEF_C * mat(gram[m, high], gram[m, :, high])
        ).astype(BF16)
        poly[m, low, high] = poly[m, high, low].T
    else:
        for cols in HALVES:
            x_it[m, :, cols] = (
                COEF_A * x_it[m, :, cols].astype(F32) + mat(poly[m], x_it[m, :, cols])
            ).astype(BF16)


def memory_kernel(
    schedule, keys, values, rates, queries, weights, gate, gain,
    layer_out, new_weights,
    k_v, v_v, w_v, rate_v, gate_v, gain_v, q_buf, r_out, r_in,
    loc, c_recv, part, x_recv, z_part, z_recv, full, x_it, gram, poly, dg_v,
    in_sem, q_ss, q_rs, r_ss, r_rs, c_ss, c_rs, x_ss, x_rs, z_ss, z_rs, y_ss, y_rs, a_ss, a_rs, f_ss, f_rs, e_ss, e_rs,
):
    ctx, head = lax.axis_index("ctx"), lax.axis_index("head")
    xi, zi, core = ctx // 8, (ctx // 2) % 4, ctx % 2

    def at(x, z, c):
        return (x * 8 + z * 2 + c, head)

    def x_other(d):
        return (xi + d) % 4

    def z_other(d):
        return (zi + d) % 4

    sibling = at(xi, zi, 1 - core)
    heads_other = [(head + d) % HEADS for d in range(1, HEADS)]

    def remote(src, dst, ss, rs, target):
        return pltpu.make_async_remote_copy(
            src_ref=src, dst_ref=dst, send_sem=ss, recv_sem=rs,
            device_id=target, device_id_type=pl.DeviceIdType.MESH,
        )

    loads = [
        pltpu.make_async_copy(keys, k_v, in_sem.at[0]),
        pltpu.make_async_copy(weights.at[0, 0], w_v.at[0], in_sem.at[1]),
        pltpu.make_async_copy(weights.at[0, 1], w_v.at[1], in_sem.at[2]),
        pltpu.make_async_copy(values, v_v, in_sem.at[3]),
        pltpu.make_async_copy(weights.at[0, 2], w_v.at[2], in_sem.at[4]),
        pltpu.make_async_copy(
            queries.at[:, pl.ds(pl.multiple_of(head * DH, DH), DH)], q_buf.at[head], in_sem.at[5]
        ),
        pltpu.make_async_copy(gate, gate_v, in_sem.at[6]),
        pltpu.make_async_copy(rates, rate_v, in_sem.at[7]),
        pltpu.make_async_copy(gain, gain_v, in_sem.at[8]),
    ]
    for i in (0, 1, 2, 7, 3):
        loads[i].start()

    barrier = pltpu.get_barrier_semaphore()
    partners = [sibling] + [at(x_other(d), zi, core) for d in (1, 2, 3)]
    partners += [at(xi, z_other(d), core) for d in (1, 2, 3)] + [(ctx, h) for h in heads_other]
    for partner in partners:
        pl.semaphore_signal(barrier, inc=1, device_id=partner, device_id_type=pl.DeviceIdType.MESH)
    for i in (4, 5, 6, 8):
        loads[i].start()

    live, copies = {}, {}

    def greet(_):
        pl.semaphore_wait(barrier, len(partners))

    def columns(own):
        half = core if own else 1 - core
        return pl.ds(pl.multiple_of(half * 256, 256), 256)

    def grad_two(own):
        cols = columns(own)
        if not own:
            loads[0].wait()
            loads[1].wait()
        g_one = mat(k_v[...], w_v[0, :, cols]) * SCALE
        if not own:
            loads[2].wait()
        g_three = mat(k_v[...], w_v[1, :, cols]) * SCALE
        sig = jax.nn.sigmoid(g_one)
        hidden = (g_one * sig * g_three).astype(BF16)
        if not own:
            loads[7].wait()
            loads[3].wait()
            rate_col = jnp.broadcast_to(rate_v[...], (128, DH)).T
            rate_wide = jnp.concatenate([rate_col] * 4, axis=1)
            live["grad_out"] = (-(rate_wide * v_v[...].astype(F32))).astype(BF16)
        loc[2, cols, :] = (mat(hidden, live["grad_out"], TN) * SCALE).astype(BF16)
        live[own] = g_one, g_three, sig

    def grad_hidden(own):
        if not own:
            loads[4].wait()
        cols = columns(own)
        g_one, g_three, sig = live[own]
        d_hidden = mat(live["grad_out"], w_v[2, cols, :], NT) * SCALE
        dg_v[0, :, cols] = (d_hidden * g_three * sig * (1.0 + g_one * (1.0 - sig))).astype(BF16)
        dg_v[1, :, cols] = (d_hidden * (g_one * sig)).astype(BF16)

    def grad_one_three(mine):
        m = core if mine else 1 - core
        loc[m] = (mat(k_v[...], dg_v[m], TN) * SCALE).astype(BF16)

    def start(key, copy):
        copy.start()
        copies.setdefault(key, []).append(copy)

    def arrived(key):
        for copy in copies[key]:
            copy.wait_recv()

    def rows_of(piece, c):
        if piece == 2:
            return loc.at[2, pl.ds(pl.multiple_of(c * 256, 256), 256)]
        return loc.at[c, pl.ds(piece * 256, 256)]

    def core_send(m):
        start(("c", m), remote(rows_of(m, 1 - core), c_recv.at[m], c_ss.at[m], c_rs.at[m], sibling))

    def block_of(piece, *at_block):
        return full.at[(0, core, *at_block) if piece == 2 else (1, piece, *at_block)]

    def x_send(m):
        arrived(("c", m))
        mine = rows_of(m, core)[...].astype(F32)
        part[m] = (mine + c_recv[m].astype(F32)).astype(BF16).reshape(4, 64, DH)
        for d in (1, 3, 2):
            start(("x", m), remote(
                part.at[m, x_other(d)], x_recv.at[m, d - 1], x_ss.at[m, d - 1], x_rs.at[m, d - 1],
                at(x_other(d), zi, core),
            ))

    def z_send(m):
        arrived(("x", m))
        total = part[m, xi].astype(F32)
        for d in range(3):
            total = total + x_recv[m, d].astype(F32)
        z_part[m] = total.astype(BF16).reshape(4, 16, DH)
        for d in (1, 3, 2):
            start(("z", m), remote(
                z_part.at[m, z_other(d)], z_recv.at[m, d - 1], z_ss.at[m, d - 1], z_rs.at[m, d - 1],
                at(xi, z_other(d), core),
            ))

    def y_send(m):
        arrived(("z", m))
        total = z_part[m, zi].astype(F32)
        for d in range(3):
            total = total + z_recv[m, d].astype(F32)
        block = block_of(m, xi, zi)
        block[...] = total.astype(BF16)
        for d in (1, 3, 2):
            start(("y", m), remote(block, block, y_ss.at[m, d - 1], y_rs.at[m, d - 1], at(xi, z_other(d), core)))

    def a_send(m):
        arrived(("y", m))
        block = block_of(m, xi)
        for d in (1, 3, 2):
            start(("a", m), remote(block, block, a_ss.at[m, d - 1], a_rs.at[m, d - 1], at(x_other(d), zi, core)))
        if m == 2:
            start(("f", m), remote(block, block, f_ss.at[0], f_rs.at[0], sibling))

    def forward_two(_):
        for i, d in enumerate((1, 3, 2)):
            copies["a", 2][i].wait_recv()
            block = block_of(2, (xi + 4 - d) % 4)
            start(("f", 2), remote(block, block, f_ss.at[d], f_rs.at[d], sibling))

    def normalise(slot):
        for key in (("f", 2),) if slot == 0 else (("a", 0), ("a", 1)):
            arrived(key)
        grad = full[slot].reshape(DH, DH).astype(F32)
        norm = jnp.sqrt(jnp.sum(grad * grad)) + 1e-07
        x_it[slot] = (grad / norm).astype(BF16)

    def update(_):
        new_weights[0, 2] = (w_v[2].astype(F32) - STEP_SIZE * x_it[0].astype(F32)).astype(BF16)

    def update_own(half):
        cols = HALVES[half]
        last = (COEF_A * x_it[1, :, cols].astype(F32) + mat(poly[1], x_it[1, :, cols])).astype(BF16)
        new_weights[0, core, :, cols] = (w_v[core, :, cols].astype(F32) - STEP_SIZE * last.astype(F32)).astype(BF16)
        block = new_weights.at[0, core, :, cols]
        start("e", remote(block, block, e_ss.at[half], e_rs.at[half], sibling))

    def query_send(_):
        for d, h in enumerate(heads_other):
            start("q", remote(
                queries.at[:, pl.ds(pl.multiple_of(h * DH, DH), DH)], q_buf.at[head], q_ss.at[d], q_rs.at[d], (ctx, h)
            ))

    def readout(_):
        loads[5].wait()
        arrived("q")
        q_rows = q_buf[...].reshape(HEADS * 64, DH)
        r_one = mat(q_rows, w_v[0]) * SCALE
        r_three = mat(q_rows, w_v[1]) * SCALE
        hq = (r_one * jax.nn.sigmoid(r_one) * r_three).astype(BF16)
        r_out[...] = (mat(hq, w_v[2]) * SCALE).astype(BF16).reshape(HEADS, 64, DH)

    def read_send(_):
        for d, h in enumerate(heads_other):
            start("r", remote(r_out.at[h], r_in.at[head], r_ss.at[d], r_rs.at[d], (ctx, h)))
        r_in[head] = r_out[head]

    def read_wait(_):
        loads[6].wait()
        loads[8].wait()
        arrived("r")

    def finish_read(h):
        cols = slice(h * DH, (h + 1) * DH)
        read = r_in[h].astype(F32)
        mean_sq = jnp.mean(read * read, axis=-1, keepdims=True)
        gated = gate_v[:, cols].astype(F32)
        layer_out[:, cols] = (
            read * lax.rsqrt(mean_sq + 1e-06) * gain_v[:, cols] * (gated * jax.nn.sigmoid(gated))
        ).astype(BF16)

    work = {
        "greet": greet, "grad_two": grad_two, "grad_hidden": grad_hidden, "grad_one_three": grad_one_three, "core_send": core_send, "x_send": x_send, "z_send": z_send,
        "y_send": y_send, "a_send": a_send, "forward_two": forward_two, "normalise": normalise, "update": update, "update_own": update_own, "read_wait": read_wait, "query_send": query_send, "readout": readout,
        "read_send": read_send, "finish_read": finish_read,
    }
    steps = [0, 0]
    for name, m in schedule:
        if name == "orthogonal":
            orthogonal_step(m, steps[m] % 3, x_it, gram, poly)
            steps[m] += 1
        else:
            work[name](m)

    arrived("e")
    for group in copies.values():
        for copy in group:
            copy.wait_send()


def closing_kernel(layer, weights, layer_out, new_weights, sems):
    copies = [pltpu.make_async_copy(weights.at[0, m], new_weights.at[0, m], sems.at[m]) for m in range(3)]
    copies.append(pltpu.make_async_copy(layer, layer_out, sems.at[3]))
    for copy in copies:
        copy.start()
    for copy in copies:
        copy.wait()


def local(keys, values, rates, queries, fast_weights, gate, gain):
    operands = (keys, values, rates, queries, fast_weights, gate, gain.reshape(1, HEADS * DH))
    vmem = pl.BlockSpec(memory_space=pltpu.VMEM)
    hbm = pl.BlockSpec(memory_space=pltpu.HBM)
    dma = pltpu.SemaphoreType.DMA
    results = pl.pallas_call(
        functools.partial(memory_kernel, SCHEDULE),
        name="memory_layer",
        out_shape=(
            pltpu.VMEM((64, HEADS * DH), BF16),
            pltpu.VMEM((1, 3, DH, DH), BF16),
        ),
        in_specs=[hbm] * 7,
        out_specs=(vmem, vmem),
        scratch_shapes=[
            pltpu.VMEM((512, DH), BF16),
            pltpu.VMEM((512, DH), BF16),
            pltpu.VMEM((3, DH, DH), BF16),
            pltpu.VMEM((1, 512), F32),
            pltpu.VMEM((64, HEADS * DH), BF16),
            pltpu.VMEM((1, HEADS * DH), F32),
            pltpu.VMEM((HEADS, 64, DH), BF16),
            pltpu.VMEM((HEADS, 64, DH), BF16),
            pltpu.VMEM((HEADS, 64, DH), BF16),
            pltpu.VMEM((3, DH, DH), BF16),
            pltpu.VMEM((3, 256, DH), BF16),
            pltpu.VMEM((3, 4, 64, DH), BF16),
            pltpu.VMEM((3, 3, 64, DH), BF16),
            pltpu.VMEM((3, 4, 16, DH), BF16),
            pltpu.VMEM((3, 3, 16, DH), BF16),
            pltpu.VMEM((2, 2, 4, 4, 16, DH), BF16),
            pltpu.VMEM((2, DH, DH), BF16),
            pltpu.VMEM((2, DH, DH), BF16),
            pltpu.VMEM((2, DH, DH), BF16),
            pltpu.VMEM((2, DH, DH), BF16),
            dma((9,)),
            dma((7,)), dma((7,)), dma((7,)), dma((7,)),
            dma((3,)), dma((3,)),
            dma((3, 3)), dma((3, 3)), dma((3, 3)), dma((3, 3)), dma((3, 3)), dma((3, 3)), dma((3, 3)), dma((3, 3)),
            dma((4,)), dma((4,)), dma((2,)), dma((2,)),
        ],
        compiler_params=pltpu.CompilerParams(
            collective_id=0, has_side_effects=True, vmem_limit_bytes=44 * 2**20
        ),
    )(*(pltpu.with_memory_space_constraint(operand, pltpu.HBM) for operand in operands))
    return pl.pallas_call(
        closing_kernel,
        name="closing_copy",
        out_shape=(
            jax.ShapeDtypeStruct((64, HEADS * DH), BF16),
            jax.ShapeDtypeStruct((1, 3, DH, DH), BF16),
        ),
        in_specs=[vmem] * 2,
        out_specs=(hbm, hbm),
        scratch_shapes=[dma((4,))],
        compiler_params=pltpu.CompilerParams(vmem_limit_bytes=16 * 2**20),
    )(*(pltpu.with_memory_space_constraint(result, pltpu.VMEM) for result in results))


def solution(mesh):
    in_specs = (
        P("ctx", "head"),
        P("ctx", "head"),
        P("head", "ctx"),
        P(("ctx", "head"), None),
        P("head", None, None, None),
        P(("ctx", "head"), None),
        P(),
    )
    out_specs = (P(("ctx", "head"), None), P("head", None, None, None))
    return jax.shard_map(local, mesh=mesh, in_specs=in_specs, out_specs=out_specs, check_vma=False)
```

```python
import functools

import jax
import jax.numpy as jnp
from jax import lax
from jax.experimental import pallas as pl
from jax.experimental.pallas import tpu as pltpu
from jax.sharding import PartitionSpec as P

NS_STEPS = 5
DH = 512
HEADS = 8
SCALE = DH ** (-0.5)
COEF_A, COEF_B, COEF_C = 3.4445, -4.775, 2.0315
STEP_SIZE = 0.4 * DH ** 0.5
F32, BF16 = jnp.float32, jnp.bfloat16
NT = (((1,), (1,)), ((), ()))
TN = (((0,), (0,)), ((), ()))
NN = (((1,), (0,)), ((), ()))


def mat(left, right, dims=NN):
    return lax.dot_general(left, right, dims, preferred_element_type=F32)


SCHEDULE = (
    ("grad_two", 0), ("greet", 0), ("core_send", 2), ("query_send", 0), ("grad_two", 1), ("x_send", 2),
    ("grad_hidden", 0), ("grad_hidden", 1), ("grad_one_three", 0), ("core_send", 0), ("core_send", 1),
    ("grad_one_three", 1), ("x_send", 0), ("x_send", 1), ("z_send", 2), ("z_send", 0), ("z_send", 1), ("y_send", 2),
    ("readout", 0), ("y_send", 0), ("y_send", 1), ("read_send", 0), ("a_send", 2), ("a_send", 0), ("a_send", 1),
    ("forward_two", 2), ("normalise", 0), ("orthogonal", 0), ("orthogonal", 0), ("orthogonal", 0), ("orthogonal", 0),
    ("orthogonal", 0), ("orthogonal", 0), ("orthogonal", 0), ("orthogonal", 0), ("orthogonal", 0), ("normalise", 1),
    ("orthogonal", 1), ("orthogonal", 0), ("orthogonal", 1), ("orthogonal", 0), ("orthogonal", 1), ("orthogonal", 0),
    ("orthogonal", 1), ("orthogonal", 0), ("orthogonal", 1), ("orthogonal", 0), ("orthogonal", 1), ("orthogonal", 0),
    ("orthogonal", 1), ("update", 0), ("orthogonal", 1), ("orthogonal", 1), ("orthogonal", 1), ("orthogonal", 1),
    ("orthogonal", 1), ("orthogonal", 1), ("orthogonal", 1), ("update_own", 0), ("update_own", 1), ("read_wait", 0),
    ("finish_read", 0), ("finish_read", 1), ("finish_read", 2), ("finish_read", 3), ("finish_read", 4),
    ("finish_read", 5), ("finish_read", 6), ("finish_read", 7),
)
HALVES = (slice(0, 256), slice(256, 512))


def orthogonal_step(m, phase, x_it, gram, poly):
    low, high = HALVES
    if phase == 0:
        gram[m, :, low] = mat(x_it[m], x_it[m, low, :], NT).astype(BF16)
        gram[m, high, high] = mat(x_it[m, high], x_it[m, high, :], NT).astype(BF16)
        gram[m, low, high] = gram[m, high, low].T
    elif phase == 1:
        poly[m, :, low] = (
            COEF_B * gram[m, :, low].astype(F32) + COEF_C * mat(gram[m], gram[m, :, low])
        ).astype(BF16)
        poly[m, high, high] = (
            COEF_B * gram[m, high, high].astype(F32) + COEF_C * mat(gram[m, high], gram[m, :, high])
        ).astype(BF16)
        poly[m, low, high] = poly[m, high, low].T
    else:
        for cols in HALVES:
            x_it[m, :, cols] = (
                COEF_A * x_it[m, :, cols].astype(F32) + mat(poly[m], x_it[m, :, cols])
            ).astype(BF16)


def memory_kernel(
    schedule, keys, values, rates, queries, weights, gate, gain,
    layer_out, new_weights,
    k_v, v_v, w_v, rate_v, gate_v, gain_v, q_buf, r_out, r_in,
    loc, c_recv, part, x_recv, z_part, z_recv, full, x_it, gram, poly, dg_v,
    in_sem, q_ss, q_rs, r_ss, r_rs, c_ss, c_rs, x_ss, x_rs, z_ss, z_rs, y_ss, y_rs, a_ss, a_rs, f_ss, f_rs, e_ss, e_rs,
):
    ctx, head = lax.axis_index("ctx"), lax.axis_index("head")
    xi, zi, core = ctx // 8, (ctx // 2) % 4, ctx % 2

    def at(x, z, c):
        return (x * 8 + z * 2 + c, head)

    def x_other(d):
        return (xi + d) % 4

    def z_other(d):
        return (zi + d) % 4

    sibling = at(xi, zi, 1 - core)
    heads_other = [(head + d) % HEADS for d in range(1, HEADS)]

    def remote(src, dst, ss, rs, target):
        return pltpu.make_async_remote_copy(
            src_ref=src, dst_ref=dst, send_sem=ss, recv_sem=rs,
            device_id=target, device_id_type=pl.DeviceIdType.MESH,
        )

    loads = [
        pltpu.make_async_copy(keys, k_v, in_sem.at[0]),
        pltpu.make_async_copy(weights.at[0, 0], w_v.at[0], in_sem.at[1]),
        pltpu.make_async_copy(weights.at[0, 1], w_v.at[1], in_sem.at[2]),
        pltpu.make_async_copy(values, v_v, in_sem.at[3]),
        pltpu.make_async_copy(weights.at[0, 2], w_v.at[2], in_sem.at[4]),
        pltpu.make_async_copy(
            queries.at[:, pl.ds(pl.multiple_of(head * DH, DH), DH)], q_buf.at[head], in_sem.at[5]
        ),
        pltpu.make_async_copy(gate, gate_v, in_sem.at[6]),
        pltpu.make_async_copy(rates, rate_v, in_sem.at[7]),
        pltpu.make_async_copy(gain, gain_v, in_sem.at[8]),
    ]
    for i in (0, 1, 2, 7, 3):
        loads[i].start()

    barrier = pltpu.get_barrier_semaphore()
    partners = [sibling] + [at(x_other(d), zi, core) for d in (1, 2, 3)]
    partners += [at(xi, z_other(d), core) for d in (1, 2, 3)] + [(ctx, h) for h in heads_other]
    for partner in partners:
        pl.semaphore_signal(barrier, inc=1, device_id=partner, device_id_type=pl.DeviceIdType.MESH)
    for i in (4, 5, 6, 8):
        loads[i].start()

    live, copies = {}, {}

    def greet(_):
        pl.semaphore_wait(barrier, len(partners))

    def columns(own):
        half = core if own else 1 - core
        return pl.ds(pl.multiple_of(half * 256, 256), 256)

    def grad_two(own):
        cols = columns(own)
        if not own:
            loads[0].wait()
            loads[1].wait()
        g_one = mat(k_v[...], w_v[0, :, cols]) * SCALE
        if not own:
            loads[2].wait()
        g_three = mat(k_v[...], w_v[1, :, cols]) * SCALE
        sig = jax.nn.sigmoid(g_one)
        hidden = (g_one * sig * g_three).astype(BF16)
        if not own:
            loads[7].wait()
            loads[3].wait()
            rate_col = jnp.broadcast_to(rate_v[...], (128, DH)).T
            rate_wide = jnp.concatenate([rate_col] * 4, axis=1)
            live["grad_out"] = (-(rate_wide * v_v[...].astype(F32))).astype(BF16)
        loc[2, cols, :] = (mat(hidden, live["grad_out"], TN) * SCALE).astype(BF16)
        live[own] = g_one, g_three, sig

    def grad_hidden(own):
        if not own:
            loads[4].wait()
        cols = columns(own)
        g_one, g_three, sig = live[own]
        d_hidden = mat(live["grad_out"], w_v[2, cols, :], NT) * SCALE
        dg_v[0, :, cols] = (d_hidden * g_three * sig * (1.0 + g_one * (1.0 - sig))).astype(BF16)
        dg_v[1, :, cols] = (d_hidden * (g_one * sig)).astype(BF16)

    def grad_one_three(mine):
        m = core if mine else 1 - core
        loc[m] = (mat(k_v[...], dg_v[m], TN) * SCALE).astype(BF16)

    def start(key, copy):
        copy.start()
        copies.setdefault(key, []).append(copy)

    def arrived(key):
        for copy in copies[key]:
            copy.wait_recv()

    def rows_of(piece, c):
        if piece == 2:
            return loc.at[2, pl.ds(pl.multiple_of(c * 256, 256), 256)]
        return loc.at[c, pl.ds(piece * 256, 256)]

    def core_send(m):
        start(("c", m), remote(rows_of(m, 1 - core), c_recv.at[m], c_ss.at[m], c_rs.at[m], sibling))

    def block_of(piece, *at_block):
        return full.at[(0, core, *at_block) if piece == 2 else (1, piece, *at_block)]

    def x_send(m):
        arrived(("c", m))
        mine = rows_of(m, core)[...].astype(F32)
        part[m] = (mine + c_recv[m].astype(F32)).astype(BF16).reshape(4, 64, DH)
        for d in (1, 3, 2):
            start(("x", m), remote(
                part.at[m, x_other(d)], x_recv.at[m, d - 1], x_ss.at[m, d - 1], x_rs.at[m, d - 1],
                at(x_other(d), zi, core),
            ))

    def z_send(m):
        arrived(("x", m))
        total = part[m, xi].astype(F32)
        for d in range(3):
            total = total + x_recv[m, d].astype(F32)
        z_part[m] = total.astype(BF16).reshape(4, 16, DH)
        for d in (1, 3, 2):
            start(("z", m), remote(
                z_part.at[m, z_other(d)], z_recv.at[m, d - 1], z_ss.at[m, d - 1], z_rs.at[m, d - 1],
                at(xi, z_other(d), core),
            ))

    def y_send(m):
        arrived(("z", m))
        total = z_part[m, zi].astype(F32)
        for d in range(3):
            total = total + z_recv[m, d].astype(F32)
        block = block_of(m, xi, zi)
        block[...] = total.astype(BF16)
        for d in (1, 3, 2):
            start(("y", m), remote(block, block, y_ss.at[m, d - 1], y_rs.at[m, d - 1], at(xi, z_other(d), core)))

    def a_send(m):
        arrived(("y", m))
        block = block_of(m, xi)
        for d in (1, 3, 2):
            start(("a", m), remote(block, block, a_ss.at[m, d - 1], a_rs.at[m, d - 1], at(x_other(d), zi, core)))
        if m == 2:
            start(("f", m), remote(block, block, f_ss.at[0], f_rs.at[0], sibling))

    def forward_two(_):
        for i, d in enumerate((1, 3, 2)):
            copies["a", 2][i].wait_recv()
            block = block_of(2, (xi + 4 - d) % 4)
            start(("f", 2), remote(block, block, f_ss.at[d], f_rs.at[d], sibling))

    def normalise(slot):
        for key in (("f", 2),) if slot == 0 else (("a", 0), ("a", 1)):
            arrived(key)
        grad = full[slot].reshape(DH, DH).astype(F32)
        norm = jnp.sqrt(jnp.sum(grad * grad)) + 1e-07
        x_it[slot] = (grad / norm).astype(BF16)

    def update(_):
        new_weights[0, 2] = (w_v[2].astype(F32) - STEP_SIZE * x_it[0].astype(F32)).astype(BF16)

    def update_own(half):
        cols = HALVES[half]
        last = (COEF_A * x_it[1, :, cols].astype(F32) + mat(poly[1], x_it[1, :, cols])).astype(BF16)
        new_weights[0, core, :, cols] = (w_v[core, :, cols].astype(F32) - STEP_SIZE * last.astype(F32)).astype(BF16)
        block = new_weights.at[0, core, :, cols]
        start("e", remote(block, block, e_ss.at[half], e_rs.at[half], sibling))

    def query_send(_):
        for d, h in enumerate(heads_other):
            start("q", remote(
                queries.at[:, pl.ds(pl.multiple_of(h * DH, DH), DH)], q_buf.at[head], q_ss.at[d], q_rs.at[d], (ctx, h)
            ))

    def readout(_):
        loads[5].wait()
        arrived("q")
        q_rows = q_buf[...].reshape(HEADS * 64, DH)
        r_one = mat(q_rows, w_v[0]) * SCALE
        r_three = mat(q_rows, w_v[1]) * SCALE
        hq = (r_one * jax.nn.sigmoid(r_one) * r_three).astype(BF16)
        r_out[...] = (mat(hq, w_v[2]) * SCALE).astype(BF16).reshape(HEADS, 64, DH)

    def read_send(_):
        for d, h in enumerate(heads_other):
            start("r", remote(r_out.at[h], r_in.at[head], r_ss.at[d], r_rs.at[d], (ctx, h)))
        r_in[head] = r_out[head]

    def read_wait(_):
        loads[6].wait()
        loads[8].wait()
        arrived("r")

    def finish_read(h):
        cols = slice(h * DH, (h + 1) * DH)
        read = r_in[h].astype(F32)
        mean_sq = jnp.mean(read * read, axis=-1, keepdims=True)
        gated = gate_v[:, cols].astype(F32)
        layer_out[:, cols] = (
            read * lax.rsqrt(mean_sq + 1e-06) * gain_v[:, cols] * (gated * jax.nn.sigmoid(gated))
        ).astype(BF16)

    work = {
        "greet": greet, "grad_two": grad_two, "grad_hidden": grad_hidden, "grad_one_three": grad_one_three, "core_send": core_send, "x_send": x_send, "z_send": z_send,
        "y_send": y_send, "a_send": a_send, "forward_two": forward_two, "normalise": normalise, "update": update, "update_own": update_own, "read_wait": read_wait, "query_send": query_send, "readout": readout,
        "read_send": read_send, "finish_read": finish_read,
    }
    steps = [0, 0]
    for name, m in schedule:
        if name == "orthogonal":
            orthogonal_step(m, steps[m] % 3, x_it, gram, poly)
            steps[m] += 1
        else:
            work[name](m)

    arrived("e")
    for group in copies.values():
        for copy in group:
            copy.wait_send()


def closing_kernel(layer, weights, layer_out, new_weights, sems):
    copies = [pltpu.make_async_copy(weights.at[0, m], new_weights.at[0, m], sems.at[m]) for m in range(3)]
    copies.append(pltpu.make_async_copy(layer, layer_out, sems.at[3]))
    for copy in copies:
        copy.start()
    for copy in copies:
        copy.wait()


def local(keys, values, rates, queries, fast_weights, gate, gain):
    operands = (keys, values, rates, queries, fast_weights, gate, gain.reshape(1, HEADS * DH))
    vmem = pl.BlockSpec(memory_space=pltpu.VMEM)
    hbm = pl.BlockSpec(memory_space=pltpu.HBM)
    dma = pltpu.SemaphoreType.DMA
    results = pl.pallas_call(
        functools.partial(memory_kernel, SCHEDULE),
        name="memory_layer",
        out_shape=(
            pltpu.VMEM((64, HEADS * DH), BF16),
            pltpu.VMEM((1, 3, DH, DH), BF16),
        ),
        in_specs=[hbm] * 7,
        out_specs=(vmem, vmem),
        scratch_shapes=[
            pltpu.VMEM((512, DH), BF16),
            pltpu.VMEM((512, DH), BF16),
            pltpu.VMEM((3, DH, DH), BF16),
            pltpu.VMEM((1, 512), F32),
            pltpu.VMEM((64, HEADS * DH), BF16),
            pltpu.VMEM((1, HEADS * DH), F32),
            pltpu.VMEM((HEADS, 64, DH), BF16),
            pltpu.VMEM((HEADS, 64, DH), BF16),
            pltpu.VMEM((HEADS, 64, DH), BF16),
            pltpu.VMEM((3, DH, DH), BF16),
            pltpu.VMEM((3, 256, DH), BF16),
            pltpu.VMEM((3, 4, 64, DH), BF16),
            pltpu.VMEM((3, 3, 64, DH), BF16),
            pltpu.VMEM((3, 4, 16, DH), BF16),
            pltpu.VMEM((3, 3, 16, DH), BF16),
            pltpu.VMEM((2, 2, 4, 4, 16, DH), BF16),
            pltpu.VMEM((2, DH, DH), BF16),
            pltpu.VMEM((2, DH, DH), BF16),
            pltpu.VMEM((2, DH, DH), BF16),
            pltpu.VMEM((2, DH, DH), BF16),
            dma((9,)),
            dma((7,)), dma((7,)), dma((7,)), dma((7,)),
            dma((3,)), dma((3,)),
            dma((3, 3)), dma((3, 3)), dma((3, 3)), dma((3, 3)), dma((3, 3)), dma((3, 3)), dma((3, 3)), dma((3, 3)),
            dma((4,)), dma((4,)), dma((2,)), dma((2,)),
        ],
        compiler_params=pltpu.CompilerParams(
            collective_id=0, has_side_effects=True, vmem_limit_bytes=44 * 2**20
        ),
    )(*(pltpu.with_memory_space_constraint(operand, pltpu.HBM) for operand in operands))
    return pl.pallas_call(
        closing_kernel,
        name="closing_copy",
        out_shape=(
            jax.ShapeDtypeStruct((64, HEADS * DH), BF16),
            jax.ShapeDtypeStruct((1, 3, DH, DH), BF16),
        ),
        in_specs=[vmem] * 2,
        out_specs=(hbm, hbm),
        scratch_shapes=[dma((4,))],
        compiler_params=pltpu.CompilerParams(vmem_limit_bytes=16 * 2**20),
    )(*(pltpu.with_memory_space_constraint(result, pltpu.VMEM) for result in results))


def solution(mesh):
    in_specs = (
        P("ctx", "head"),
        P("ctx", "head"),
        P("head", "ctx"),
        P(("ctx", "head"), None),
        P("head", None, None, None),
        P(("ctx", "head"), None),
        P(),
    )
    out_specs = (P(("ctx", "head"), None), P("head", None, None, None))
    return jax.shard_map(local, mesh=mesh, in_specs=in_specs, out_specs=out_specs, check_vma=False)
```

```python
import functools

import jax
import jax.numpy as jnp
from jax import lax
from jax.experimental import pallas as pl
from jax.experimental.pallas import tpu as pltpu
from jax.sharding import PartitionSpec as P

NS_STEPS = 5
DH = 512
HEADS = 8
SCALE = DH ** (-0.5)
COEF_A, COEF_B, COEF_C = 3.4445, -4.775, 2.0315
STEP_SIZE = 0.4 * DH ** 0.5
F32, BF16 = jnp.float32, jnp.bfloat16
NT = (((1,), (1,)), ((), ()))
TN = (((0,), (0,)), ((), ()))
NN = (((1,), (0,)), ((), ()))


def mat(left, right, dims=NN):
    return lax.dot_general(left, right, dims, preferred_element_type=F32)


SCHEDULE = (
    ("grad_two", 0), ("greet", 0), ("core_send", 2), ("query_send", 0), ("grad_two", 1), ("x_send", 2),
    ("grad_hidden", 0), ("grad_hidden", 1), ("grad_one_three", 0), ("core_send", 0), ("core_send", 1),
    ("grad_one_three", 1), ("x_send", 0), ("x_send", 1), ("z_send", 2), ("z_send", 0), ("z_send", 1), ("y_send", 2),
    ("readout", 0), ("y_send", 0), ("y_send", 1), ("read_send", 0), ("a_send", 2), ("a_send", 0), ("a_send", 1),
    ("forward_two", 2), ("normalise", 0), ("orthogonal", 0), ("orthogonal", 0), ("orthogonal", 0), ("orthogonal", 0),
    ("orthogonal", 0), ("orthogonal", 0), ("orthogonal", 0), ("orthogonal", 0), ("orthogonal", 0), ("normalise", 1),
    ("orthogonal", 1), ("orthogonal", 0), ("orthogonal", 1), ("orthogonal", 0), ("orthogonal", 1), ("orthogonal", 0),
    ("orthogonal", 1), ("orthogonal", 0), ("orthogonal", 1), ("orthogonal", 0), ("orthogonal", 1), ("orthogonal", 0),
    ("orthogonal", 1), ("update", 0), ("orthogonal", 1), ("orthogonal", 1), ("orthogonal", 1), ("orthogonal", 1),
    ("orthogonal", 1), ("orthogonal", 1), ("orthogonal", 1), ("update_own", 0), ("update_own", 1), ("read_wait", 0),
    ("finish_read", 0), ("finish_read", 1), ("finish_read", 2), ("finish_read", 3), ("finish_read", 4),
    ("finish_read", 5), ("finish_read", 6), ("finish_read", 7),
)
HALVES = (slice(0, 256), slice(256, 512))


def orthogonal_step(m, phase, x_it, gram, poly):
    low, high = HALVES
    if phase == 0:
        gram[m, :, low] = mat(x_it[m], x_it[m, low, :], NT).astype(BF16)
        gram[m, high, high] = mat(x_it[m, high], x_it[m, high, :], NT).astype(BF16)
        gram[m, low, high] = gram[m, high, low].T
    elif phase == 1:
        poly[m, :, low] = (
            COEF_B * gram[m, :, low].astype(F32) + COEF_C * mat(gram[m], gram[m, :, low])
        ).astype(BF16)
        poly[m, high, high] = (
            COEF_B * gram[m, high, high].astype(F32) + COEF_C * mat(gram[m, high], gram[m, :, high])
        ).astype(BF16)
        poly[m, low, high] = poly[m, high, low].T
    else:
        for cols in HALVES:
            x_it[m, :, cols] = (
                COEF_A * x_it[m, :, cols].astype(F32) + mat(poly[m], x_it[m, :, cols])
            ).astype(BF16)


def memory_kernel(
    schedule, keys, values, rates, queries, weights, gate, gain,
    layer_out, new_weights,
    k_v, v_v, w_v, rate_v, gate_v, gain_v, q_buf, r_out, r_in,
    loc, c_recv, part, x_recv, z_part, z_recv, full, x_it, gram, poly, dg_v,
    in_sem, q_ss, q_rs, r_ss, r_rs, c_ss, c_rs, x_ss, x_rs, z_ss, z_rs, y_ss, y_rs, a_ss, a_rs, f_ss, f_rs, e_ss, e_rs,
):
    ctx, head = lax.axis_index("ctx"), lax.axis_index("head")
    xi, zi, core = ctx // 8, (ctx // 2) % 4, ctx % 2

    def at(x, z, c):
        return (x * 8 + z * 2 + c, head)

    def x_other(d):
        return (xi + d) % 4

    def z_other(d):
        return (zi + d) % 4

    sibling = at(xi, zi, 1 - core)
    heads_other = [(head + d) % HEADS for d in range(1, HEADS)]

    def remote(src, dst, ss, rs, target):
        return pltpu.make_async_remote_copy(
            src_ref=src, dst_ref=dst, send_sem=ss, recv_sem=rs,
            device_id=target, device_id_type=pl.DeviceIdType.MESH,
        )

    loads = [
        pltpu.make_async_copy(keys, k_v, in_sem.at[0]),
        pltpu.make_async_copy(weights.at[0, 0], w_v.at[0], in_sem.at[1]),
        pltpu.make_async_copy(weights.at[0, 1], w_v.at[1], in_sem.at[2]),
        pltpu.make_async_copy(values, v_v, in_sem.at[3]),
        pltpu.make_async_copy(weights.at[0, 2], w_v.at[2], in_sem.at[4]),
        pltpu.make_async_copy(
            queries.at[:, pl.ds(pl.multiple_of(head * DH, DH), DH)], q_buf.at[head], in_sem.at[5]
        ),
        pltpu.make_async_copy(gate, gate_v, in_sem.at[6]),
        pltpu.make_async_copy(rates, rate_v, in_sem.at[7]),
        pltpu.make_async_copy(gain, gain_v, in_sem.at[8]),
    ]
    for i in (0, 1, 2, 7, 3):
        loads[i].start()

    barrier = pltpu.get_barrier_semaphore()
    partners = [sibling] + [at(x_other(d), zi, core) for d in (1, 2, 3)]
    partners += [at(xi, z_other(d), core) for d in (1, 2, 3)] + [(ctx, h) for h in heads_other]
    for partner in partners:
        pl.semaphore_signal(barrier, inc=1, device_id=partner, device_id_type=pl.DeviceIdType.MESH)
    for i in (4, 5, 6, 8):
        loads[i].start()

    live, copies = {}, {}

    def greet(_):
        pl.semaphore_wait(barrier, len(partners))

    def columns(own):
        half = core if own else 1 - core
        return pl.ds(pl.multiple_of(half * 256, 256), 256)

    def grad_two(own):
        cols = columns(own)
        if not own:
            loads[0].wait()
            loads[1].wait()
        g_one = mat(k_v[...], w_v[0, :, cols]) * SCALE
        if not own:
            loads[2].wait()
        g_three = mat(k_v[...], w_v[1, :, cols]) * SCALE
        sig = jax.nn.sigmoid(g_one)
        hidden = (g_one * sig * g_three).astype(BF16)
        if not own:
            loads[7].wait()
            loads[3].wait()
            rate_col = jnp.broadcast_to(rate_v[...], (128, DH)).T
            rate_wide = jnp.concatenate([rate_col] * 4, axis=1)
            live["grad_out"] = (-(rate_wide * v_v[...].astype(F32))).astype(BF16)
        loc[2, cols, :] = (mat(hidden, live["grad_out"], TN) * SCALE).astype(BF16)
        live[own] = g_one, g_three, sig

    def grad_hidden(own):
        if not own:
            loads[4].wait()
        cols = columns(own)
        g_one, g_three, sig = live[own]
        d_hidden = mat(live["grad_out"], w_v[2, cols, :], NT) * SCALE
        dg_v[0, :, cols] = (d_hidden * g_three * sig * (1.0 + g_one * (1.0 - sig))).astype(BF16)
        dg_v[1, :, cols] = (d_hidden * (g_one * sig)).astype(BF16)

    def grad_one_three(mine):
        m = core if mine else 1 - core
        loc[m] = (mat(k_v[...], dg_v[m], TN) * SCALE).astype(BF16)

    def start(key, copy):
        copy.start()
        copies.setdefault(key, []).append(copy)

    def arrived(key):
        for copy in copies[key]:
            copy.wait_recv()

    def rows_of(piece, c):
        if piece == 2:
            return loc.at[2, pl.ds(pl.multiple_of(c * 256, 256), 256)]
        return loc.at[c, pl.ds(piece * 256, 256)]

    def core_send(m):
        start(("c", m), remote(rows_of(m, 1 - core), c_recv.at[m], c_ss.at[m], c_rs.at[m], sibling))

    def block_of(piece, *at_block):
        return full.at[(0, core, *at_block) if piece == 2 else (1, piece, *at_block)]

    def x_send(m):
        arrived(("c", m))
        mine = rows_of(m, core)[...].astype(F32)
        part[m] = (mine + c_recv[m].astype(F32)).astype(BF16).reshape(4, 64, DH)
        for d in (2, 1, 3):
            start(("x", m), remote(
                part.at[m, x_other(d)], x_recv.at[m, d - 1], x_ss.at[m, d - 1], x_rs.at[m, d - 1],
                at(x_other(d), zi, core),
            ))

    def z_send(m):
        arrived(("x", m))
        total = part[m, xi].astype(F32)
        for d in range(3):
            total = total + x_recv[m, d].astype(F32)
        z_part[m] = total.astype(BF16).reshape(4, 16, DH)
        for d in (2, 1, 3):
            start(("z", m), remote(
                z_part.at[m, z_other(d)], z_recv.at[m, d - 1], z_ss.at[m, d - 1], z_rs.at[m, d - 1],
                at(xi, z_other(d), core),
            ))

    def y_send(m):
        arrived(("z", m))
        total = z_part[m, zi].astype(F32)
        for d in range(3):
            total = total + z_recv[m, d].astype(F32)
        block = block_of(m, xi, zi)
        block[...] = total.astype(BF16)
        for d in (2, 1, 3):
            start(("y", m), remote(block, block, y_ss.at[m, d - 1], y_rs.at[m, d - 1], at(xi, z_other(d), core)))

    def a_send(m):
        arrived(("y", m))
        block = block_of(m, xi)
        for d in (2, 1, 3):
            start(("a", m), remote(block, block, a_ss.at[m, d - 1], a_rs.at[m, d - 1], at(x_other(d), zi, core)))
        if m == 2:
            start(("f", m), remote(block, block, f_ss.at[0], f_rs.at[0], sibling))

    def forward_two(_):
        for i, d in enumerate((2, 1, 3)):
            copies["a", 2][i].wait_recv()
            block = block_of(2, (xi + 4 - d) % 4)
            start(("f", 2), remote(block, block, f_ss.at[d], f_rs.at[d], sibling))

    def normalise(slot):
        for key in (("f", 2),) if slot == 0 else (("a", 0), ("a", 1)):
            arrived(key)
        grad = full[slot].reshape(DH, DH).astype(F32)
        norm = jnp.sqrt(jnp.sum(grad * grad)) + 1e-07
        x_it[slot] = (grad / norm).astype(BF16)

    def update(_):
        new_weights[0, 2] = (w_v[2].astype(F32) - STEP_SIZE * x_it[0].astype(F32)).astype(BF16)

    def update_own(half):
        cols = HALVES[half]
        last = (COEF_A * x_it[1, :, cols].astype(F32) + mat(poly[1], x_it[1, :, cols])).astype(BF16)
        new_weights[0, core, :, cols] = (w_v[core, :, cols].astype(F32) - STEP_SIZE * last.astype(F32)).astype(BF16)
        block = new_weights.at[0, core, :, cols]
        start("e", remote(block, block, e_ss.at[half], e_rs.at[half], sibling))

    def query_send(_):
        for d, h in enumerate(heads_other):
            start("q", remote(
                queries.at[:, pl.ds(pl.multiple_of(h * DH, DH), DH)], q_buf.at[head], q_ss.at[d], q_rs.at[d], (ctx, h)
            ))

    def readout(_):
        loads[5].wait()
        arrived("q")
        q_rows = q_buf[...].reshape(HEADS * 64, DH)
        r_one = mat(q_rows, w_v[0]) * SCALE
        r_three = mat(q_rows, w_v[1]) * SCALE
        hq = (r_one * jax.nn.sigmoid(r_one) * r_three).astype(BF16)
        r_out[...] = (mat(hq, w_v[2]) * SCALE).astype(BF16).reshape(HEADS, 64, DH)

    def read_send(_):
        for d, h in enumerate(heads_other):
            start("r", remote(r_out.at[h], r_in.at[head], r_ss.at[d], r_rs.at[d], (ctx, h)))
        r_in[head] = r_out[head]

    def read_wait(_):
        loads[6].wait()
        loads[8].wait()
        arrived("r")

    def finish_read(h):
        cols = slice(h * DH, (h + 1) * DH)
        read = r_in[h].astype(F32)
        mean_sq = jnp.mean(read * read, axis=-1, keepdims=True)
        gated = gate_v[:, cols].astype(F32)
        layer_out[:, cols] = (
            read * lax.rsqrt(mean_sq + 1e-06) * gain_v[:, cols] * (gated * jax.nn.sigmoid(gated))
        ).astype(BF16)

    work = {
        "greet": greet, "grad_two": grad_two, "grad_hidden": grad_hidden, "grad_one_three": grad_one_three, "core_send": core_send, "x_send": x_send, "z_send": z_send,
        "y_send": y_send, "a_send": a_send, "forward_two": forward_two, "normalise": normalise, "update": update, "update_own": update_own, "read_wait": read_wait, "query_send": query_send, "readout": readout,
        "read_send": read_send, "finish_read": finish_read,
    }
    steps = [0, 0]
    for name, m in schedule:
        if name == "orthogonal":
            orthogonal_step(m, steps[m] % 3, x_it, gram, poly)
            steps[m] += 1
        else:
            work[name](m)

    arrived("e")
    for group in copies.values():
        for copy in group:
            copy.wait_send()


def closing_kernel(layer, weights, layer_out, new_weights, sems):
    copies = [pltpu.make_async_copy(weights.at[0, m], new_weights.at[0, m], sems.at[m]) for m in range(3)]
    copies.append(pltpu.make_async_copy(layer, layer_out, sems.at[3]))
    for copy in copies:
        copy.start()
    for copy in copies:
        copy.wait()


def local(keys, values, rates, queries, fast_weights, gate, gain):
    operands = (keys, values, rates, queries, fast_weights, gate, gain.reshape(1, HEADS * DH))
    vmem = pl.BlockSpec(memory_space=pltpu.VMEM)
    hbm = pl.BlockSpec(memory_space=pltpu.HBM)
    dma = pltpu.SemaphoreType.DMA
    results = pl.pallas_call(
        functools.partial(memory_kernel, SCHEDULE),
        name="memory_layer",
        out_shape=(
            pltpu.VMEM((64, HEADS * DH), BF16),
            pltpu.VMEM((1, 3, DH, DH), BF16),
        ),
        in_specs=[hbm] * 7,
        out_specs=(vmem, vmem),
        scratch_shapes=[
            pltpu.VMEM((512, DH), BF16),
            pltpu.VMEM((512, DH), BF16),
            pltpu.VMEM((3, DH, DH), BF16),
            pltpu.VMEM((1, 512), F32),
            pltpu.VMEM((64, HEADS * DH), BF16),
            pltpu.VMEM((1, HEADS * DH), F32),
            pltpu.VMEM((HEADS, 64, DH), BF16),
            pltpu.VMEM((HEADS, 64, DH), BF16),
            pltpu.VMEM((HEADS, 64, DH), BF16),
            pltpu.VMEM((3, DH, DH), BF16),
            pltpu.VMEM((3, 256, DH), BF16),
            pltpu.VMEM((3, 4, 64, DH), BF16),
            pltpu.VMEM((3, 3, 64, DH), BF16),
            pltpu.VMEM((3, 4, 16, DH), BF16),
            pltpu.VMEM((3, 3, 16, DH), BF16),
            pltpu.VMEM((2, 2, 4, 4, 16, DH), BF16),
            pltpu.VMEM((2, DH, DH), BF16),
            pltpu.VMEM((2, DH, DH), BF16),
            pltpu.VMEM((2, DH, DH), BF16),
            pltpu.VMEM((2, DH, DH), BF16),
            dma((9,)),
            dma((7,)), dma((7,)), dma((7,)), dma((7,)),
            dma((3,)), dma((3,)),
            dma((3, 3)), dma((3, 3)), dma((3, 3)), dma((3, 3)), dma((3, 3)), dma((3, 3)), dma((3, 3)), dma((3, 3)),
            dma((4,)), dma((4,)), dma((2,)), dma((2,)),
        ],
        compiler_params=pltpu.CompilerParams(
            collective_id=0, has_side_effects=True, vmem_limit_bytes=44 * 2**20
        ),
    )(*(pltpu.with_memory_space_constraint(operand, pltpu.HBM) for operand in operands))
    return pl.pallas_call(
        closing_kernel,
        name="closing_copy",
        out_shape=(
            jax.ShapeDtypeStruct((64, HEADS * DH), BF16),
            jax.ShapeDtypeStruct((1, 3, DH, DH), BF16),
        ),
        in_specs=[vmem] * 2,
        out_specs=(hbm, hbm),
        scratch_shapes=[dma((4,))],
        compiler_params=pltpu.CompilerParams(vmem_limit_bytes=16 * 2**20),
    )(*(pltpu.with_memory_space_constraint(result, pltpu.VMEM) for result in results))


def solution(mesh):
    in_specs = (
        P("ctx", "head"),
        P("ctx", "head"),
        P("head", "ctx"),
        P(("ctx", "head"), None),
        P("head", None, None, None),
        P(("ctx", "head"), None),
        P(),
    )
    out_specs = (P(("ctx", "head"), None), P("head", None, None, None))
    return jax.shard_map(local, mesh=mesh, in_specs=in_specs, out_specs=out_specs, check_vma=False)
```

```python
import functools

import jax
import jax.numpy as jnp
from jax import lax
from jax.experimental import pallas as pl
from jax.experimental.pallas import tpu as pltpu
from jax.sharding import PartitionSpec as P

NS_STEPS = 5
DH = 512
HEADS = 8
SCALE = DH ** (-0.5)
COEF_A, COEF_B, COEF_C = 3.4445, -4.775, 2.0315
STEP_SIZE = 0.4 * DH ** 0.5
F32, BF16 = jnp.float32, jnp.bfloat16
NT = (((1,), (1,)), ((), ()))
TN = (((0,), (0,)), ((), ()))
NN = (((1,), (0,)), ((), ()))


def mat(left, right, dims=NN):
    return lax.dot_general(left, right, dims, preferred_element_type=F32)


SCHEDULE = (
    ("grad_two", 0), ("greet", 0), ("core_send", 2), ("query_send", 0), ("grad_two", 1), ("x_send", 2),
    ("grad_hidden", 0), ("grad_hidden", 1), ("grad_one_three", 0), ("core_send", 0), ("core_send", 1),
    ("grad_one_three", 1), ("x_send", 0), ("x_send", 1), ("z_send", 2), ("z_send", 0), ("z_send", 1), ("y_send", 2),
    ("readout", 0), ("y_send", 0), ("y_send", 1), ("read_send", 0), ("a_send", 2), ("a_send", 0), ("a_send", 1),
    ("forward_two", 2), ("normalise", 0), ("orthogonal", 0), ("orthogonal", 0), ("orthogonal", 0), ("orthogonal", 0),
    ("orthogonal", 0), ("orthogonal", 0), ("orthogonal", 0), ("orthogonal", 0), ("orthogonal", 0), ("normalise", 1),
    ("orthogonal", 1), ("orthogonal", 0), ("orthogonal", 1), ("orthogonal", 0), ("orthogonal", 1), ("orthogonal", 0),
    ("orthogonal", 1), ("orthogonal", 0), ("orthogonal", 1), ("orthogonal", 0), ("orthogonal", 1), ("orthogonal", 0),
    ("orthogonal", 1), ("update", 0), ("orthogonal", 1), ("orthogonal", 1), ("orthogonal", 1), ("orthogonal", 1),
    ("orthogonal", 1), ("orthogonal", 1), ("orthogonal", 1), ("update_own", 0), ("update_own", 1), ("read_wait", 0),
    ("finish_read", 0), ("finish_read", 1), ("finish_read", 2), ("finish_read", 3), ("finish_read", 4),
    ("finish_read", 5), ("finish_read", 6), ("finish_read", 7),
)
HALVES = (slice(0, 256), slice(256, 512))


def orthogonal_step(m, phase, x_it, gram, poly):
    low, high = HALVES
    if phase == 0:
        gram[m, :, low] = mat(x_it[m], x_it[m, low, :], NT).astype(BF16)
        gram[m, high, high] = mat(x_it[m, high], x_it[m, high, :], NT).astype(BF16)
        gram[m, low, high] = gram[m, high, low].T
    elif phase == 1:
        poly[m, :, low] = (
            COEF_B * gram[m, :, low].astype(F32) + COEF_C * mat(gram[m], gram[m, :, low])
        ).astype(BF16)
        poly[m, high, high] = (
            COEF_B * gram[m, high, high].astype(F32) + COEF_C * mat(gram[m, high], gram[m, :, high])
        ).astype(BF16)
        poly[m, low, high] = poly[m, high, low].T
    else:
        for cols in HALVES:
            x_it[m, :, cols] = (
                COEF_A * x_it[m, :, cols].astype(F32) + mat(poly[m], x_it[m, :, cols])
            ).astype(BF16)


def memory_kernel(
    schedule, keys, values, rates, queries, weights, gate, gain,
    layer_out, new_weights,
    k_v, v_v, w_v, rate_v, gate_v, gain_v, q_buf, r_out, r_in,
    loc, c_recv, part, x_recv, z_part, z_recv, full, x_it, gram, poly, dg_v,
    in_sem, q_ss, q_rs, r_ss, r_rs, c_ss, c_rs, x_ss, x_rs, z_ss, z_rs, y_ss, y_rs, a_ss, a_rs, f_ss, f_rs, e_ss, e_rs,
):
    ctx, head = lax.axis_index("ctx"), lax.axis_index("head")
    xi, zi, core = ctx // 8, (ctx // 2) % 4, ctx % 2

    def at(x, z, c):
        return (x * 8 + z * 2 + c, head)

    def x_other(d):
        return (xi + d) % 4

    def z_other(d):
        return (zi + d) % 4

    sibling = at(xi, zi, 1 - core)
    heads_other = [(head + d) % HEADS for d in (4, 5, 3, 2, 6, 1, 7)]

    def remote(src, dst, ss, rs, target):
        return pltpu.make_async_remote_copy(
            src_ref=src, dst_ref=dst, send_sem=ss, recv_sem=rs,
            device_id=target, device_id_type=pl.DeviceIdType.MESH,
        )

    loads = [
        pltpu.make_async_copy(keys, k_v, in_sem.at[0]),
        pltpu.make_async_copy(weights.at[0, 0], w_v.at[0], in_sem.at[1]),
        pltpu.make_async_copy(weights.at[0, 1], w_v.at[1], in_sem.at[2]),
        pltpu.make_async_copy(values, v_v, in_sem.at[3]),
        pltpu.make_async_copy(weights.at[0, 2], w_v.at[2], in_sem.at[4]),
        pltpu.make_async_copy(
            queries.at[:, pl.ds(pl.multiple_of(head * DH, DH), DH)], q_buf.at[head], in_sem.at[5]
        ),
        pltpu.make_async_copy(gate, gate_v, in_sem.at[6]),
        pltpu.make_async_copy(rates, rate_v, in_sem.at[7]),
        pltpu.make_async_copy(gain, gain_v, in_sem.at[8]),
    ]
    for i in (0, 1, 2, 7, 3):
        loads[i].start()

    barrier = pltpu.get_barrier_semaphore()
    partners = [sibling] + [at(x_other(d), zi, core) for d in (1, 2, 3)]
    partners += [at(xi, z_other(d), core) for d in (1, 2, 3)] + [(ctx, h) for h in heads_other]
    for partner in partners:
        pl.semaphore_signal(barrier, inc=1, device_id=partner, device_id_type=pl.DeviceIdType.MESH)
    for i in (4, 5, 6, 8):
        loads[i].start()

    live, copies = {}, {}

    def greet(_):
        pl.semaphore_wait(barrier, len(partners))

    def columns(own):
        half = core if own else 1 - core
        return pl.ds(pl.multiple_of(half * 256, 256), 256)

    def grad_two(own):
        cols = columns(own)
        if not own:
            loads[0].wait()
            loads[1].wait()
        g_one = mat(k_v[...], w_v[0, :, cols]) * SCALE
        if not own:
            loads[2].wait()
        g_three = mat(k_v[...], w_v[1, :, cols]) * SCALE
        sig = jax.nn.sigmoid(g_one)
        hidden = (g_one * sig * g_three).astype(BF16)
        if not own:
            loads[7].wait()
            loads[3].wait()
            rate_col = jnp.broadcast_to(rate_v[...], (128, DH)).T
            rate_wide = jnp.concatenate([rate_col] * 4, axis=1)
            live["grad_out"] = (-(rate_wide * v_v[...].astype(F32))).astype(BF16)
        loc[2, cols, :] = (mat(hidden, live["grad_out"], TN) * SCALE).astype(BF16)
        live[own] = g_one, g_three, sig

    def grad_hidden(own):
        if not own:
            loads[4].wait()
        cols = columns(own)
        g_one, g_three, sig = live[own]
        d_hidden = mat(live["grad_out"], w_v[2, cols, :], NT) * SCALE
        dg_v[0, :, cols] = (d_hidden * g_three * sig * (1.0 + g_one * (1.0 - sig))).astype(BF16)
        dg_v[1, :, cols] = (d_hidden * (g_one * sig)).astype(BF16)

    def grad_one_three(mine):
        m = core if mine else 1 - core
        loc[m] = (mat(k_v[...], dg_v[m], TN) * SCALE).astype(BF16)

    def start(key, copy):
        copy.start()
        copies.setdefault(key, []).append(copy)

    def arrived(key):
        for copy in copies[key]:
            copy.wait_recv()

    def rows_of(piece, c):
        if piece == 2:
            return loc.at[2, pl.ds(pl.multiple_of(c * 256, 256), 256)]
        return loc.at[c, pl.ds(piece * 256, 256)]

    def core_send(m):
        start(("c", m), remote(rows_of(m, 1 - core), c_recv.at[m], c_ss.at[m], c_rs.at[m], sibling))

    def block_of(piece, *at_block):
        return full.at[(0, core, *at_block) if piece == 2 else (1, piece, *at_block)]

    def x_send(m):
        arrived(("c", m))
        mine = rows_of(m, core)[...].astype(F32)
        part[m] = (mine + c_recv[m].astype(F32)).astype(BF16).reshape(4, 64, DH)
        for d in (2, 1, 3):
            start(("x", m), remote(
                part.at[m, x_other(d)], x_recv.at[m, d - 1], x_ss.at[m, d - 1], x_rs.at[m, d - 1],
                at(x_other(d), zi, core),
            ))

    def z_send(m):
        arrived(("x", m))
        total = part[m, xi].astype(F32)
        for d in range(3):
            total = total + x_recv[m, d].astype(F32)
        z_part[m] = total.astype(BF16).reshape(4, 16, DH)
        for d in (2, 1, 3):
            start(("z", m), remote(
                z_part.at[m, z_other(d)], z_recv.at[m, d - 1], z_ss.at[m, d - 1], z_rs.at[m, d - 1],
                at(xi, z_other(d), core),
            ))

    def y_send(m):
        arrived(("z", m))
        total = z_part[m, zi].astype(F32)
        for d in range(3):
            total = total + z_recv[m, d].astype(F32)
        block = block_of(m, xi, zi)
        block[...] = total.astype(BF16)
        for d in (2, 1, 3):
            start(("y", m), remote(block, block, y_ss.at[m, d - 1], y_rs.at[m, d - 1], at(xi, z_other(d), core)))

    def a_send(m):
        arrived(("y", m))
        block = block_of(m, xi)
        for d in (2, 1, 3):
            start(("a", m), remote(block, block, a_ss.at[m, d - 1], a_rs.at[m, d - 1], at(x_other(d), zi, core)))
        if m == 2:
            start(("f", m), remote(block, block, f_ss.at[0], f_rs.at[0], sibling))

    def forward_two(_):
        for i, d in enumerate((2, 1, 3)):
            copies["a", 2][i].wait_recv()
            block = block_of(2, (xi + 4 - d) % 4)
            start(("f", 2), remote(block, block, f_ss.at[d], f_rs.at[d], sibling))

    def normalise(slot):
        for key in (("f", 2),) if slot == 0 else (("a", 0), ("a", 1)):
            arrived(key)
        grad = full[slot].reshape(DH, DH).astype(F32)
        norm = jnp.sqrt(jnp.sum(grad * grad)) + 1e-07
        x_it[slot] = (grad / norm).astype(BF16)

    def update(_):
        new_weights[0, 2] = (w_v[2].astype(F32) - STEP_SIZE * x_it[0].astype(F32)).astype(BF16)

    def update_own(half):
        cols = HALVES[half]
        for i, rows in enumerate(HALVES):
            last = COEF_A * x_it[1, rows, cols].astype(F32) + mat(poly[1, rows], x_it[1, :, cols])
            last = last.astype(BF16).astype(F32)
            new_weights[0, core, rows, cols] = (w_v[core, rows, cols].astype(F32) - STEP_SIZE * last).astype(BF16)
            block = new_weights.at[0, core, rows, cols]
            start("e", remote(block, block, e_ss.at[2 * half + i], e_rs.at[2 * half + i], sibling))

    def query_send(_):
        for d, h in enumerate(heads_other):
            start("q", remote(
                queries.at[:, pl.ds(pl.multiple_of(h * DH, DH), DH)], q_buf.at[head], q_ss.at[d], q_rs.at[d], (ctx, h)
            ))

    def readout(_):
        loads[5].wait()
        arrived("q")
        q_rows = q_buf[...].reshape(HEADS * 64, DH)
        r_one = mat(q_rows, w_v[0]) * SCALE
        r_three = mat(q_rows, w_v[1]) * SCALE
        hq = (r_one * jax.nn.sigmoid(r_one) * r_three).astype(BF16)
        r_out[...] = (mat(hq, w_v[2]) * SCALE).astype(BF16).reshape(HEADS, 64, DH)

    def read_send(_):
        for d, h in enumerate(heads_other):
            start("r", remote(r_out.at[h], r_in.at[head], r_ss.at[d], r_rs.at[d], (ctx, h)))
        r_in[head] = r_out[head]

    def read_wait(_):
        loads[6].wait()
        loads[8].wait()
        arrived("r")

    def finish_read(h):
        cols = slice(h * DH, (h + 1) * DH)
        read = r_in[h].astype(F32)
        mean_sq = jnp.mean(read * read, axis=-1, keepdims=True)
        gated = gate_v[:, cols].astype(F32)
        layer_out[:, cols] = (
            read * lax.rsqrt(mean_sq + 1e-06) * gain_v[:, cols] * (gated * jax.nn.sigmoid(gated))
        ).astype(BF16)

    work = {
        "greet": greet, "grad_two": grad_two, "grad_hidden": grad_hidden, "grad_one_three": grad_one_three, "core_send": core_send, "x_send": x_send, "z_send": z_send,
        "y_send": y_send, "a_send": a_send, "forward_two": forward_two, "normalise": normalise, "update": update, "update_own": update_own, "read_wait": read_wait, "query_send": query_send, "readout": readout,
        "read_send": read_send, "finish_read": finish_read,
    }
    steps = [0, 0]
    for name, m in schedule:
        if name == "orthogonal":
            orthogonal_step(m, steps[m] % 3, x_it, gram, poly)
            steps[m] += 1
        else:
            work[name](m)

    arrived("e")
    for group in copies.values():
        for copy in group:
            copy.wait_send()


def closing_kernel(layer, weights, layer_out, new_weights, sems):
    copies = [pltpu.make_async_copy(weights.at[0, m], new_weights.at[0, m], sems.at[m]) for m in range(3)]
    copies.append(pltpu.make_async_copy(layer, layer_out, sems.at[3]))
    for copy in copies:
        copy.start()
    for copy in copies:
        copy.wait()


def local(keys, values, rates, queries, fast_weights, gate, gain):
    operands = (keys, values, rates, queries, fast_weights, gate, gain.reshape(1, HEADS * DH))
    vmem = pl.BlockSpec(memory_space=pltpu.VMEM)
    hbm = pl.BlockSpec(memory_space=pltpu.HBM)
    dma = pltpu.SemaphoreType.DMA
    results = pl.pallas_call(
        functools.partial(memory_kernel, SCHEDULE),
        name="memory_layer",
        out_shape=(
            pltpu.VMEM((64, HEADS * DH), BF16),
            pltpu.VMEM((1, 3, DH, DH), BF16),
        ),
        in_specs=[hbm] * 7,
        out_specs=(vmem, vmem),
        scratch_shapes=[
            pltpu.VMEM((512, DH), BF16),
            pltpu.VMEM((512, DH), BF16),
            pltpu.VMEM((3, DH, DH), BF16),
            pltpu.VMEM((1, 512), F32),
            pltpu.VMEM((64, HEADS * DH), BF16),
            pltpu.VMEM((1, HEADS * DH), F32),
            pltpu.VMEM((HEADS, 64, DH), BF16),
            pltpu.VMEM((HEADS, 64, DH), BF16),
            pltpu.VMEM((HEADS, 64, DH), BF16),
            pltpu.VMEM((3, DH, DH), BF16),
            pltpu.VMEM((3, 256, DH), BF16),
            pltpu.VMEM((3, 4, 64, DH), BF16),
            pltpu.VMEM((3, 3, 64, DH), BF16),
            pltpu.VMEM((3, 4, 16, DH), BF16),
            pltpu.VMEM((3, 3, 16, DH), BF16),
            pltpu.VMEM((2, 2, 4, 4, 16, DH), BF16),
            pltpu.VMEM((2, DH, DH), BF16),
            pltpu.VMEM((2, DH, DH), BF16),
            pltpu.VMEM((2, DH, DH), BF16),
            pltpu.VMEM((2, DH, DH), BF16),
            dma((9,)),
            dma((7,)), dma((7,)), dma((7,)), dma((7,)),
            dma((3,)), dma((3,)),
            dma((3, 3)), dma((3, 3)), dma((3, 3)), dma((3, 3)), dma((3, 3)), dma((3, 3)), dma((3, 3)), dma((3, 3)),
            dma((4,)), dma((4,)), dma((4,)), dma((4,)),
        ],
        compiler_params=pltpu.CompilerParams(
            collective_id=0, has_side_effects=True, vmem_limit_bytes=44 * 2**20
        ),
    )(*(pltpu.with_memory_space_constraint(operand, pltpu.HBM) for operand in operands))
    return pl.pallas_call(
        closing_kernel,
        name="closing_copy",
        out_shape=(
            jax.ShapeDtypeStruct((64, HEADS * DH), BF16),
            jax.ShapeDtypeStruct((1, 3, DH, DH), BF16),
        ),
        in_specs=[vmem] * 2,
        out_specs=(hbm, hbm),
        scratch_shapes=[dma((4,))],
        compiler_params=pltpu.CompilerParams(vmem_limit_bytes=16 * 2**20),
    )(*(pltpu.with_memory_space_constraint(result, pltpu.VMEM) for result in results))


def solution(mesh):
    in_specs = (
        P("ctx", "head"),
        P("ctx", "head"),
        P("head", "ctx"),
        P(("ctx", "head"), None),
        P("head", None, None, None),
        P(("ctx", "head"), None),
        P(),
    )
    out_specs = (P(("ctx", "head"), None), P("head", None, None, None))
    return jax.shard_map(local, mesh=mesh, in_specs=in_specs, out_specs=out_specs, check_vma=False)
```

```python
import functools

import jax
import jax.numpy as jnp
from jax import lax
from jax.experimental import pallas as pl
from jax.experimental.pallas import tpu as pltpu
from jax.sharding import PartitionSpec as P

NS_STEPS = 5
DH = 512
HEADS = 8
SCALE = DH ** (-0.5)
COEF_A, COEF_B, COEF_C = 3.4445, -4.775, 2.0315
STEP_SIZE = 0.4 * DH ** 0.5
F32, BF16 = jnp.float32, jnp.bfloat16
NT = (((1,), (1,)), ((), ()))
TN = (((0,), (0,)), ((), ()))
NN = (((1,), (0,)), ((), ()))


def mat(left, right, dims=NN):
    return lax.dot_general(left, right, dims, preferred_element_type=F32)


SCHEDULE = (
    ("grad_two", 0), ("greet", 0), ("core_send", 2), ("query_send", 0), ("grad_two", 1), ("x_send", 2),
    ("grad_hidden", 0), ("grad_hidden", 1), ("grad_one_three", 0), ("core_send", 0), ("core_send", 1),
    ("grad_one_three", 1), ("x_send", 0), ("x_send", 1), ("z_send", 2), ("z_send", 0), ("z_send", 1), ("y_send", 2),
    ("readout", 0), ("y_send", 0), ("y_send", 1), ("read_send", 0), ("a_send", 2), ("a_send", 0), ("a_send", 1),
    ("forward_two", 2), ("normalise", 0), ("orthogonal", 0), ("orthogonal", 0), ("orthogonal", 0), ("orthogonal", 0),
    ("orthogonal", 0), ("orthogonal", 0), ("orthogonal", 0), ("orthogonal", 0), ("orthogonal", 0), ("normalise", 1),
    ("orthogonal", 1), ("orthogonal", 0), ("orthogonal", 1), ("orthogonal", 0), ("orthogonal", 1), ("orthogonal", 0),
    ("orthogonal", 1), ("orthogonal", 0), ("orthogonal", 1), ("orthogonal", 0), ("orthogonal", 1), ("orthogonal", 0),
    ("orthogonal", 1), ("update", 0), ("orthogonal", 1), ("orthogonal", 1), ("orthogonal", 1), ("orthogonal", 1),
    ("orthogonal", 1), ("orthogonal", 1), ("orthogonal", 1), ("update_own", 0), ("update_own", 1), ("read_wait", 0),
    ("finish_read", 0), ("finish_read", 1), ("finish_read", 2), ("finish_read", 3), ("finish_read", 4),
    ("finish_read", 5), ("finish_read", 6), ("finish_read", 7),
)
HALVES = (slice(0, 256), slice(256, 512))


def orthogonal_step(m, phase, x_it, gram, poly):
    low, high = HALVES
    if phase == 0:
        gram[m, :, low] = mat(x_it[m], x_it[m, low, :], NT).astype(BF16)
        gram[m, high, high] = mat(x_it[m, high], x_it[m, high, :], NT).astype(BF16)
        gram[m, low, high] = gram[m, high, low].T
    elif phase == 1:
        poly[m, :, low] = (
            COEF_B * gram[m, :, low].astype(F32) + COEF_C * mat(gram[m], gram[m, :, low])
        ).astype(BF16)
        poly[m, high, high] = (
            COEF_B * gram[m, high, high].astype(F32) + COEF_C * mat(gram[m, high], gram[m, :, high])
        ).astype(BF16)
        poly[m, low, high] = poly[m, high, low].T
    else:
        for cols in HALVES:
            x_it[m, :, cols] = (
                COEF_A * x_it[m, :, cols].astype(F32) + mat(poly[m], x_it[m, :, cols])
            ).astype(BF16)


def memory_kernel(
    schedule, keys, values, rates, queries, weights, gate, gain,
    layer_out, new_weights,
    k_v, v_v, w_v, rate_v, gate_v, gain_v, q_buf, r_out, r_in,
    loc, c_recv, part, x_recv, z_part, z_recv, full, x_it, gram, poly, dg_v,
    in_sem, q_ss, q_rs, r_ss, r_rs, c_ss, c_rs, x_ss, x_rs, z_ss, z_rs, y_ss, y_rs, a_ss, a_rs, f_ss, f_rs, e_ss, e_rs,
):
    ctx, head = lax.axis_index("ctx"), lax.axis_index("head")
    xi, zi, core = ctx // 8, (ctx // 2) % 4, ctx % 2

    def at(x, z, c):
        return (x * 8 + z * 2 + c, head)

    def x_other(d):
        return (xi + d) % 4

    def z_other(d):
        return (zi + d) % 4

    sibling = at(xi, zi, 1 - core)
    heads_other = [(head + d) % HEADS for d in range(1, HEADS)]

    def remote(src, dst, ss, rs, target):
        return pltpu.make_async_remote_copy(
            src_ref=src, dst_ref=dst, send_sem=ss, recv_sem=rs,
            device_id=target, device_id_type=pl.DeviceIdType.MESH,
        )

    loads = [
        pltpu.make_async_copy(keys, k_v, in_sem.at[0]),
        pltpu.make_async_copy(weights.at[0, 0], w_v.at[0], in_sem.at[1]),
        pltpu.make_async_copy(weights.at[0, 1], w_v.at[1], in_sem.at[2]),
        pltpu.make_async_copy(values, v_v, in_sem.at[3]),
        pltpu.make_async_copy(weights.at[0, 2], w_v.at[2], in_sem.at[4]),
        pltpu.make_async_copy(
            queries.at[:, pl.ds(pl.multiple_of(head * DH, DH), DH)], q_buf.at[head], in_sem.at[5]
        ),
        pltpu.make_async_copy(gate, gate_v, in_sem.at[6]),
        pltpu.make_async_copy(rates, rate_v, in_sem.at[7]),
        pltpu.make_async_copy(gain, gain_v, in_sem.at[8]),
    ]
    for i in (0, 1, 2, 7, 3):
        loads[i].start()

    barrier = pltpu.get_barrier_semaphore()
    partners = [sibling] + [at(x_other(d), zi, core) for d in (1, 2, 3)]
    partners += [at(xi, z_other(d), core) for d in (1, 2, 3)] + [(ctx, h) for h in heads_other]
    for partner in partners:
        pl.semaphore_signal(barrier, inc=1, device_id=partner, device_id_type=pl.DeviceIdType.MESH)
    for i in (4, 5, 6, 8):
        loads[i].start()

    live, copies = {}, {}

    def greet(_):
        pl.semaphore_wait(barrier, len(partners))

    def columns(own):
        half = core if own else 1 - core
        return pl.ds(pl.multiple_of(half * 256, 256), 256)

    def grad_two(own):
        cols = columns(own)
        if not own:
            loads[0].wait()
            loads[1].wait()
        g_one = mat(k_v[...], w_v[0, :, cols]) * SCALE
        if not own:
            loads[2].wait()
        g_three = mat(k_v[...], w_v[1, :, cols]) * SCALE
        sig = jax.nn.sigmoid(g_one)
        hidden = (g_one * sig * g_three).astype(BF16)
        if not own:
            loads[7].wait()
            loads[3].wait()
            rate_col = jnp.broadcast_to(rate_v[...], (128, DH)).T
            rate_wide = jnp.concatenate([rate_col] * 4, axis=1)
            live["grad_out"] = (-(rate_wide * v_v[...].astype(F32))).astype(BF16)
        loc[2, cols, :] = (mat(hidden, live["grad_out"], TN) * SCALE).astype(BF16)
        live[own] = g_one, g_three, sig

    def grad_hidden(own):
        if not own:
            loads[4].wait()
        cols = columns(own)
        g_one, g_three, sig = live[own]
        d_hidden = mat(live["grad_out"], w_v[2, cols, :], NT) * SCALE
        dg_v[0, :, cols] = (d_hidden * g_three * sig * (1.0 + g_one * (1.0 - sig))).astype(BF16)
        dg_v[1, :, cols] = (d_hidden * (g_one * sig)).astype(BF16)

    def grad_one_three(mine):
        m = core if mine else 1 - core
        loc[m] = (mat(k_v[...], dg_v[m], TN) * SCALE).astype(BF16)

    def start(key, copy):
        copy.start()
        copies.setdefault(key, []).append(copy)

    def arrived(key):
        for copy in copies[key]:
            copy.wait_recv()

    def rows_of(piece, c):
        if piece == 2:
            return loc.at[2, pl.ds(pl.multiple_of(c * 256, 256), 256)]
        return loc.at[c, pl.ds(piece * 256, 256)]

    def core_send(m):
        start(("c", m), remote(rows_of(m, 1 - core), c_recv.at[m], c_ss.at[m], c_rs.at[m], sibling))

    def block_of(piece, *at_block):
        return full.at[(0, core, *at_block) if piece == 2 else (1, piece, *at_block)]

    def x_send(m):
        arrived(("c", m))
        mine = rows_of(m, core)[...].astype(F32)
        part[m] = (mine + c_recv[m].astype(F32)).astype(BF16).reshape(4, 64, DH)
        for d in (2, 1, 3):
            start(("x", m), remote(
                part.at[m, x_other(d)], x_recv.at[m, d - 1], x_ss.at[m, d - 1], x_rs.at[m, d - 1],
                at(x_other(d), zi, core),
            ))

    def z_send(m):
        arrived(("x", m))
        total = part[m, xi].astype(F32)
        for d in range(3):
            total = total + x_recv[m, d].astype(F32)
        z_part[m] = total.astype(BF16).reshape(4, 16, DH)
        for d in (2, 1, 3):
            start(("z", m), remote(
                z_part.at[m, z_other(d)], z_recv.at[m, d - 1], z_ss.at[m, d - 1], z_rs.at[m, d - 1],
                at(xi, z_other(d), core),
            ))

    def y_send(m):
        arrived(("z", m))
        total = z_part[m, zi].astype(F32)
        for d in range(3):
            total = total + z_recv[m, d].astype(F32)
        block = block_of(m, xi, zi)
        block[...] = total.astype(BF16)
        for d in (2, 1, 3):
            start(("y", m), remote(block, block, y_ss.at[m, d - 1], y_rs.at[m, d - 1], at(xi, z_other(d), core)))

    def a_send(m):
        arrived(("y", m))
        block = block_of(m, xi)
        for d in (2, 1, 3):
            start(("a", m), remote(block, block, a_ss.at[m, d - 1], a_rs.at[m, d - 1], at(x_other(d), zi, core)))
        if m == 2:
            start(("f", m), remote(block, block, f_ss.at[0], f_rs.at[0], sibling))

    def forward_two(_):
        for i, d in enumerate((2, 1, 3)):
            copies["a", 2][i].wait_recv()
            block = block_of(2, (xi + 4 - d) % 4)
            start(("f", 2), remote(block, block, f_ss.at[d], f_rs.at[d], sibling))

    def normalise(slot):
        keys_of = (("f", 2),) if slot == 0 else (("a", 0), ("a", 1))
        total = 0.0
        for i, rows in enumerate(HALVES):
            if i < len(keys_of):
                arrived(keys_of[i])
            grad = full[slot, i].reshape(256, DH).astype(F32)
            total = total + jnp.sum(grad * grad)
        inverse = 1.0 / (jnp.sqrt(total) + 1e-07)
        for i, rows in enumerate(HALVES):
            x_it[slot, rows, :] = (full[slot, i].reshape(256, DH).astype(F32) * inverse).astype(BF16)

    def update(_):
        new_weights[0, 2] = (w_v[2].astype(F32) - STEP_SIZE * x_it[0].astype(F32)).astype(BF16)

    def update_own(half):
        cols = HALVES[half]
        last = (COEF_A * x_it[1, :, cols].astype(F32) + mat(poly[1], x_it[1, :, cols])).astype(BF16)
        new_weights[0, core, :, cols] = (w_v[core, :, cols].astype(F32) - STEP_SIZE * last.astype(F32)).astype(BF16)
        block = new_weights.at[0, core, :, cols]
        start("e", remote(block, block, e_ss.at[half], e_rs.at[half], sibling))

    def query_send(_):
        for d, h in enumerate(heads_other):
            start("q", remote(
                queries.at[:, pl.ds(pl.multiple_of(h * DH, DH), DH)], q_buf.at[head], q_ss.at[d], q_rs.at[d], (ctx, h)
            ))

    def readout(_):
        loads[5].wait()
        arrived("q")
        q_rows = q_buf[...].reshape(HEADS * 64, DH)
        r_one = mat(q_rows, w_v[0]) * SCALE
        r_three = mat(q_rows, w_v[1]) * SCALE
        hq = (r_one * jax.nn.sigmoid(r_one) * r_three).astype(BF16)
        r_out[...] = (mat(hq, w_v[2]) * SCALE).astype(BF16).reshape(HEADS, 64, DH)

    def read_send(_):
        for d, h in enumerate(heads_other):
            start("r", remote(r_out.at[h], r_in.at[head], r_ss.at[d], r_rs.at[d], (ctx, h)))
        r_in[head] = r_out[head]

    def read_wait(_):
        loads[6].wait()
        loads[8].wait()
        arrived("r")

    def finish_read(h):
        cols = slice(h * DH, (h + 1) * DH)
        read = r_in[h].astype(F32)
        mean_sq = jnp.mean(read * read, axis=-1, keepdims=True)
        gated = gate_v[:, cols].astype(F32)
        layer_out[:, cols] = (
            read * lax.rsqrt(mean_sq + 1e-06) * gain_v[:, cols] * (gated * jax.nn.sigmoid(gated))
        ).astype(BF16)

    work = {
        "greet": greet, "grad_two": grad_two, "grad_hidden": grad_hidden, "grad_one_three": grad_one_three, "core_send": core_send, "x_send": x_send, "z_send": z_send,
        "y_send": y_send, "a_send": a_send, "forward_two": forward_two, "normalise": normalise, "update": update, "update_own": update_own, "read_wait": read_wait, "query_send": query_send, "readout": readout,
        "read_send": read_send, "finish_read": finish_read,
    }
    steps = [0, 0]
    for name, m in schedule:
        if name == "orthogonal":
            orthogonal_step(m, steps[m] % 3, x_it, gram, poly)
            steps[m] += 1
        else:
            work[name](m)

    arrived("e")
    for group in copies.values():
        for copy in group:
            copy.wait_send()


def closing_kernel(layer, weights, layer_out, new_weights, sems):
    copies = [pltpu.make_async_copy(weights.at[0, m], new_weights.at[0, m], sems.at[m]) for m in range(3)]
    copies.append(pltpu.make_async_copy(layer, layer_out, sems.at[3]))
    for copy in copies:
        copy.start()
    for copy in copies:
        copy.wait()


def local(keys, values, rates, queries, fast_weights, gate, gain):
    operands = (keys, values, rates, queries, fast_weights, gate, gain.reshape(1, HEADS * DH))
    vmem = pl.BlockSpec(memory_space=pltpu.VMEM)
    hbm = pl.BlockSpec(memory_space=pltpu.HBM)
    dma = pltpu.SemaphoreType.DMA
    results = pl.pallas_call(
        functools.partial(memory_kernel, SCHEDULE),
        name="memory_layer",
        out_shape=(
            pltpu.VMEM((64, HEADS * DH), BF16),
            pltpu.VMEM((1, 3, DH, DH), BF16),
        ),
        in_specs=[hbm] * 7,
        out_specs=(vmem, vmem),
        scratch_shapes=[
            pltpu.VMEM((512, DH), BF16),
            pltpu.VMEM((512, DH), BF16),
            pltpu.VMEM((3, DH, DH), BF16),
            pltpu.VMEM((1, 512), F32),
            pltpu.VMEM((64, HEADS * DH), BF16),
            pltpu.VMEM((1, HEADS * DH), F32),
            pltpu.VMEM((HEADS, 64, DH), BF16),
            pltpu.VMEM((HEADS, 64, DH), BF16),
            pltpu.VMEM((HEADS, 64, DH), BF16),
            pltpu.VMEM((3, DH, DH), BF16),
            pltpu.VMEM((3, 256, DH), BF16),
            pltpu.VMEM((3, 4, 64, DH), BF16),
            pltpu.VMEM((3, 3, 64, DH), BF16),
            pltpu.VMEM((3, 4, 16, DH), BF16),
            pltpu.VMEM((3, 3, 16, DH), BF16),
            pltpu.VMEM((2, 2, 4, 4, 16, DH), BF16),
            pltpu.VMEM((2, DH, DH), BF16),
            pltpu.VMEM((2, DH, DH), BF16),
            pltpu.VMEM((2, DH, DH), BF16),
            pltpu.VMEM((2, DH, DH), BF16),
            dma((9,)),
            dma((7,)), dma((7,)), dma((7,)), dma((7,)),
            dma((3,)), dma((3,)),
            dma((3, 3)), dma((3, 3)), dma((3, 3)), dma((3, 3)), dma((3, 3)), dma((3, 3)), dma((3, 3)), dma((3, 3)),
            dma((4,)), dma((4,)), dma((2,)), dma((2,)),
        ],
        compiler_params=pltpu.CompilerParams(
            collective_id=0, has_side_effects=True, vmem_limit_bytes=44 * 2**20
        ),
    )(*(pltpu.with_memory_space_constraint(operand, pltpu.HBM) for operand in operands))
    return pl.pallas_call(
        closing_kernel,
        name="closing_copy",
        out_shape=(
            jax.ShapeDtypeStruct((64, HEADS * DH), BF16),
            jax.ShapeDtypeStruct((1, 3, DH, DH), BF16),
        ),
        in_specs=[vmem] * 2,
        out_specs=(hbm, hbm),
        scratch_shapes=[dma((4,))],
        compiler_params=pltpu.CompilerParams(vmem_limit_bytes=16 * 2**20),
    )(*(pltpu.with_memory_space_constraint(result, pltpu.VMEM) for result in results))


def solution(mesh):
    in_specs = (
        P("ctx", "head"),
        P("ctx", "head"),
        P("head", "ctx"),
        P(("ctx", "head"), None),
        P("head", None, None, None),
        P(("ctx", "head"), None),
        P(),
    )
    out_specs = (P(("ctx", "head"), None), P("head", None, None, None))
    return jax.shard_map(local, mesh=mesh, in_specs=in_specs, out_specs=out_specs, check_vma=False)
```
